256 devices in a mesh: pair: 64 (over z, x, core), aux: 4 (over y).
Axes of the slice: x: 4, y: 4, z: 8, core: 2. Of those that a mesh axis runs over, the one named last changes fastest.
Arguments:
- ao_blocks: bfloat16 [64, 64, 16, 128, 128], P(None, 'pair', 'aux'), may hold values from -6 to 6
- block_live: int32 [64, 64], replicated, may hold values from 0 to 1, as said below
- tile_len: int32 [64], replicated, may hold values from 1 to 128, 6000 in all
- coeffs: bfloat16 [8192, 576], P('pair'), may hold values from -0.078125 to 0.078125
- metric_panel: bfloat16 [16, 32], replicated, may hold values from -1.5 to 1.5
Outputs:
- fitted: bfloat16 [32, 576, 8192], P('aux', 'pair')
The draws below stay inside these ranges and needn't reach their ends.
Inputs may be any that keep to these rules, and one draw needn't show every extreme that they name: `block_live`: entries with row block before column block are 0; the diagonal and the two block diagonals below it are 1. `tile_len`: the counts sum to 6000; some shell block holds exactly 128.
All inputs are finite; a program needn't handle non-finite values.
Results may differ from the reference program's by a relative error of at most 0.0049.
Values may be sent and summed in bfloat16 or wider, within the bound.
A program may use at most 128 MiB of HBM per device.

```python
import math
import jax
import jax.numpy as jnp
import numpy as np
from jax import lax

NBF = 6000
NOCC = 576
NT = 64
TILE = 128
SLAB = 16
QPAN = 32


def draw_block_live(key, part):
    key = jax.random.fold_in(key, 11)
    row_ids = jnp.arange(NT, dtype=jnp.int32)[:, None]
    col_ids = jnp.arange(NT, dtype=jnp.int32)[None, :]
    coin_flip = jax.random.randint(key, (NT, NT), 0, 4)
    nearby = row_ids - col_ids < 3
    alive = (row_ids >= col_ids) & (nearby | (coin_flip > 0))
    return alive.astype(jnp.int32)


def levels(stream_key, shape, pieces, low, largest):
    loudness, own = 1.0, jax.random.fold_in(stream_key, 6)
    for position, parts in pieces:
        steps = jnp.exp(jax.random.uniform(jax.random.fold_in(own, position), (parts,), jnp.float32, low / len(pieces), largest / len(pieces)))
        loudness = loudness * jnp.repeat(steps, shape[position] // parts).reshape([-1 if axis == position else 1 for axis in range(len(shape))])
    return loudness


def profile(amount, total, reach, slope):
    portions = [(1 << 20) // math.isqrt(standing ** slope) + 1 for standing in range(2, amount + 1)]
    spare, counts = total - reach - (amount - 1), [1] * (amount - 1)
    while spare > 0:
        free = [i for i in range(amount - 1) if counts[i] < reach]
        whole, left = sum([portions[i] for i in free]), spare
        for i in free:
            addition = min(reach - counts[i], max(1, left * portions[i] // whole), spare)
            counts[i] = counts[i] + addition
            spare = spare - addition
    return np.array([reach] + counts)


def uneven_parts(stream_key, count, total, bound, skew):
    if count == 2:
        one = jax.random.randint(stream_key, (), max(1, total - bound), min(bound, total - 1) + 1)
        return jnp.stack([one, total - one])
    lengths = jnp.asarray(profile(count, total, bound, skew), jnp.int32)
    couples = (count - 1) // 2
    source_of, receiver = lengths[1:1 + 2 * couples:2], lengths[2:2 + 2 * couples:2]
    margin = jnp.minimum(source_of - 1, bound - receiver)
    passed = jax.random.randint(jax.random.fold_in(stream_key, 1), (couples,), 0, 1 << 20) % (margin + 1)
    lengths = lengths.at[1:1 + 2 * couples:2].set(source_of - passed).at[2:2 + 2 * couples:2].set(receiver + passed)
    return lengths[jax.random.permutation(jax.random.fold_in(stream_key, 2), count)]


def noise(key, dims, deviation, bound, cuts=(), held_as=jnp.bfloat16):
    entries = jax.random.normal(key, dims, jnp.float32) * deviation
    if len(cuts) > 0:
        entries = levels(key, dims, cuts, -0.22, 0.18) * entries
    return jnp.clip(entries, min=-bound, max=bound).astype(held_as)


def setup_inputs(seed: int = 0) -> dict:
    seeds = jax.random.split(jax.random.key(seed), 6)
    return {
        "ao_blocks": noise(seeds[0], (NT, NT, SLAB, TILE, TILE), 1.0, 6.0, ((1, 64), (2, 4))),
        "block_live": draw_block_live(jax.random.fold_in(seeds[5], 71), 0),
        "tile_len": uneven_parts(seeds[2], NT, NBF, TILE, 0).astype(jnp.int32),
        "coeffs": noise(seeds[3], (NT * TILE, NOCC), NBF ** -0.5, 0.078125, ((0, 64),)),
        "metric_panel": noise(seeds[4], (SLAB, QPAN), SLAB ** -0.5, 1.5),
    }


def column_terms(ao_blocks, kept_blocks, valid_slots, coef_tiles, column):
    tile_ids = jnp.arange(NT, dtype=jnp.int32)
    inside = jnp.arange(TILE, dtype=jnp.int32)
    upper_rows = inside >= TILE // 2
    lower_half = inside[:, None] >= inside[None, :]
    strict_lower = inside[:, None] > inside[None, :]
    own_blocks = lax.dynamic_index_in_dim(ao_blocks, column, 1, keepdims=False)
    across_blocks = lax.dynamic_index_in_dim(ao_blocks, column, 0, keepdims=False)
    kept_own = lax.dynamic_index_in_dim(kept_blocks, column, 1, keepdims=False)
    kept_across = lax.dynamic_index_in_dim(kept_blocks, column, 0, keepdims=False)
    valid_column = lax.dynamic_index_in_dim(valid_slots, column, 0, keepdims=False)
    later_tiles = tile_ids > column
    earlier_tiles = tile_ids < column
    same_tile = tile_ids == column
    swap_own = later_tiles[:, None, None, None] & upper_rows[None, None, :, None]
    swap_across = earlier_tiles[:, None, None, None] & upper_rows[None, None, :, None]
    whole_own = jnp.where(swap_own, across_blocks, own_blocks)
    whole_across = jnp.where(swap_across, own_blocks, across_blocks)
    own_mask = (kept_own[:, None, None]
                & (later_tiles[:, None, None] | (same_tile[:, None, None] & lower_half[None]))
                & valid_slots[:, :, None] & valid_column[None, None, :])
    across_mask = (kept_across[:, None, None]
                   & (earlier_tiles[:, None, None] | (same_tile[:, None, None] & strict_lower[None]))
                   & valid_column[None, :, None] & valid_slots[:, None, :])
    zero_value = jnp.zeros((), jnp.bfloat16)
    own_part = jnp.where(own_mask[:, None], whole_own, zero_value).astype(jnp.float32)
    across_part = jnp.where(across_mask[:, None], whole_across, zero_value).astype(jnp.float32)
    coef_float = coef_tiles.astype(jnp.float32)
    first_term = jnp.einsum('mri,mprs->pis', coef_float, own_part)
    second_term = jnp.einsum('msi,mprs->pir', coef_float, across_part)
    return first_term + second_term


def reference(ao_blocks, block_live, tile_len, coeffs, metric_panel):
    tile_ids = jnp.arange(NT, dtype=jnp.int32)
    kept_blocks = (block_live > 0) & (tile_ids[:, None] >= tile_ids[None, :])
    valid_slots = jnp.arange(TILE, dtype=jnp.int32)[None, :] < tile_len[:, None]
    coef_tiles = coeffs.reshape(NT, TILE, NOCC)

    def one_column(column):
        return column_terms(ao_blocks, kept_blocks, valid_slots, coef_tiles, column)

    halves = lax.map(one_column, tile_ids)
    half_done = halves.astype(jnp.bfloat16)
    half_done = jnp.transpose(half_done, (1, 2, 0, 3)).reshape(SLAB, NOCC, NT * TILE)
    fitted = jnp.einsum('pq,pin->qin', metric_panel.astype(jnp.float32), half_done.astype(jnp.float32))
    return fitted.astype(jnp.bfloat16)
```

```python
import jax
import jax.numpy as jnp
from jax import lax
from jax.sharding import PartitionSpec as P


def receive_rows(ao_blocks, tile_ids, columns, half_size):
    later = (tile_ids[:, None] > columns[None, :])[:, :, None, None, None]
    needed = jnp.where(later, ao_blocks[:, :, :, :half_size], ao_blocks[:, :, :, half_size:])
    return lax.all_to_all(needed, "pair", split_axis=0, concat_axis=1, tiled=True)


def shards(ao_blocks, block_live, tile_len, coeffs, metric_panel):
    tile_count = ao_blocks.shape[0]
    own_count = ao_blocks.shape[1]
    slab_count = ao_blocks.shape[2]
    slot_size = ao_blocks.shape[3]
    half_size = slot_size // 2
    occ_count = coeffs.shape[1]
    first_tile = lax.axis_index("pair") * own_count
    tile_ids = jnp.arange(tile_count, dtype=jnp.int32)
    columns = first_tile + jnp.arange(own_count, dtype=jnp.int32)
    inside = jnp.arange(slot_size, dtype=jnp.int32)
    upper_rows = inside >= half_size
    lower_half = inside[:, None] >= inside[None, :]
    strict_lower = inside[:, None] > inside[None, :]
    kept_blocks = (block_live > 0) & (tile_ids[:, None] >= tile_ids[None, :])
    valid_slots = inside[None, :] < tile_len[:, None]
    valid_columns = lax.dynamic_slice_in_dim(valid_slots, first_tile, own_count, 0)
    kept_own = lax.dynamic_slice_in_dim(kept_blocks, first_tile, own_count, 1)
    kept_across = lax.dynamic_slice_in_dim(kept_blocks, first_tile, own_count, 0)
    later_tiles = tile_ids[:, None] > columns[None, :]
    same_tile = tile_ids[:, None] == columns[None, :]
    earlier_tiles = columns[:, None] > tile_ids[None, :]
    same_across = columns[:, None] == tile_ids[None, :]
    own_mask = (
        kept_own[:, :, None, None]
        & (later_tiles[:, :, None, None] | same_tile[:, :, None, None] & lower_half[None, None])
        & valid_slots[:, None, :, None]
        & valid_columns[None, :, None, :]
    )
    across_mask = (
        kept_across[:, :, None, None]
        & (
            earlier_tiles[:, :, None, None]
            | same_across[:, :, None, None] & strict_lower[None, None]
        )
        & valid_columns[:, None, :, None]
        & valid_slots[None, :, None, :]
    )
    upper_four = upper_rows[None, None, :, None]
    mask_stored = own_mask & jnp.logical_not(later_tiles[:, :, None, None] & upper_four)
    across_turned = jnp.transpose(across_mask, (1, 0, 2, 3))
    mask_mirror = across_turned & (
        jnp.transpose(earlier_tiles)[:, :, None, None] & upper_four | same_tile[:, :, None, None]
    )
    own_turned = jnp.transpose(own_mask, (1, 0, 2, 3))
    mask_arrived = own_turned[:, :, half_size:, :] & jnp.transpose(later_tiles)[:, :, None, None]
    mask_crossed = across_mask[:, :, :half_size, :] & earlier_tiles[:, :, None, None]
    zero_value = jnp.zeros((), ao_blocks.dtype)
    own_stored = jnp.where(mask_stored[:, :, None], ao_blocks, zero_value)
    own_mirror = jnp.where(mask_mirror[:, :, None], ao_blocks, zero_value)
    received = receive_rows(ao_blocks, tile_ids, columns, half_size)
    arrived = jnp.where(mask_arrived[:, :, None], received, zero_value)
    crossed = jnp.where(mask_crossed[:, :, None], received, zero_value)
    coef_rows = lax.all_gather(coeffs, "pair", axis=0, tiled=True)
    tile_span = coef_rows.shape[0] // slot_size
    coef_piece = coef_rows.reshape(tile_span, slot_size, occ_count)
    first = jnp.einsum(
        "kri,kgprs->pigs", coef_piece, own_stored, preferred_element_type=jnp.float32
    )
    partial_sum = first + jnp.einsum(
        "ksi,kgprs->pigr", coef_piece, own_mirror, preferred_element_type=jnp.float32
    )
    first = jnp.einsum(
        "kri,gkprs->pigs", coef_piece[:, half_size:, :], arrived, preferred_element_type=jnp.float32
    )
    lower_rows = jnp.einsum(
        "ksi,gkprs->pigr", coef_piece, crossed, preferred_element_type=jnp.float32
    )
    padding = jnp.zeros(lower_rows.shape[:3] + (slot_size - half_size,), jnp.float32)
    running = partial_sum + (first + jnp.concatenate([lower_rows, padding], axis=3))
    half_done = running.astype(jnp.bfloat16).reshape(slab_count, occ_count, own_count * slot_size)
    regrouped = lax.all_to_all(half_done, "pair", split_axis=1, concat_axis=2, tiled=True)
    slab = lax.all_gather(regrouped, "aux", axis=0, tiled=True)
    panel_count = metric_panel.shape[1] // lax.axis_size("aux")
    panel_metric = lax.dynamic_slice_in_dim(
        metric_panel, lax.axis_index("aux") * panel_count, panel_count, 1
    )
    fitted = jnp.einsum("pq,pin->qin", panel_metric, slab, preferred_element_type=jnp.float32)
    return fitted.astype(jnp.bfloat16)


def solution(mesh):
    in_specs = (P(None, "pair", "aux", None, None), P(), P(), P("pair", None), P())
    out_specs = P("aux", "pair", None)
    return jax.shard_map(shards, mesh=mesh, in_specs=in_specs, out_specs=out_specs, check_vma=False)
```

```python
import functools

import jax
import jax.numpy as jnp
from jax import lax
from jax.experimental import pallas as pl
from jax.experimental.pallas import tpu as pltpu
from jax.sharding import PartitionSpec as P

MESH = pl.DeviceIdType.MESH
PLANES = 8
REACH = 4
F32 = jnp.float32
BF16 = jnp.bfloat16


def exchange_kernel(peers, ao, got, send_sem, recv_sem, own_sem):
    me, aux = lax.axis_index("pair"), lax.axis_index("aux")
    plane, slot = me // peers, me % peers
    half = ao.shape[3] // 2

    def piece(tile):
        start = pl.multiple_of(jnp.where(tile > me, 0, half), half)
        return ao.at[tile, 0, :, pl.ds(start, half), :]

    def send(group, step):
        other = lax.rem(slot + step, peers)
        return pltpu.make_async_remote_copy(
            src_ref=piece(group * peers + other),
            dst_ref=got.at[group, slot],
            send_sem=send_sem.at[group, step],
            recv_sem=recv_sem.at[group, step],
            device_id=(plane * peers + other, aux),
            device_id_type=MESH,
        )

    def keep(group):
        return pltpu.make_async_copy(
            piece(group * peers + slot), got.at[group, slot], own_sem.at[group]
        )

    barrier = pltpu.get_barrier_semaphore()
    for step in range(1, peers):
        other = lax.rem(slot + step, peers)
        pl.semaphore_signal(
            barrier, inc=1, device_id=(plane * peers + other, aux), device_id_type=MESH
        )
    pl.semaphore_wait(barrier, peers - 1)

    @pl.loop(0, PLANES)
    def _(group):
        keep(group).start()
        for step in range(1, peers):
            send(group, step).start()

    @pl.loop(0, PLANES)
    def _(group):
        keep(group).wait()
        for step in range(1, peers):
            send(group, step).wait()


def exchange(ao, peers):
    tiles, _, slab, size, width = ao.shape
    return pl.pallas_call(
        functools.partial(exchange_kernel, peers),
        out_shape=jax.ShapeDtypeStruct((PLANES, peers, slab, size // 2, width), ao.dtype),
        in_specs=[pl.BlockSpec(memory_space=pl.ANY)],
        out_specs=pl.BlockSpec(memory_space=pl.ANY),
        scratch_shapes=[
            pltpu.SemaphoreType.DMA((PLANES, peers)),
            pltpu.SemaphoreType.DMA((PLANES, peers)),
            pltpu.SemaphoreType.DMA((PLANES,)),
        ],
        compiler_params=pltpu.CompilerParams(collective_id=0, has_side_effects=True),
        cost_estimate=pl.CostEstimate(flops=0, bytes_accessed=180_000_000, transcendentals=0),
    )(ao)


def partial_kernel(peers, place, live, coef_group, coef_plane, ao, got, out, direct, mirror):
    plane, me = place[0], place[1]
    step = pl.program_id(0)
    group = lax.rem(plane + 1 + step, PLANES)
    slab, size = ao.shape[2], ao.shape[3]
    half = size // 2
    target = group * peers + lax.rem(me, peers)
    row = lax.broadcasted_iota(jnp.int32, (size, size), 0)
    col = lax.broadcasted_iota(jnp.int32, (size, size), 1)

    def one(cond):
        return jnp.where(cond, 1.0, 0.0).astype(F32)

    def kept(first, second):
        return one(live[jnp.maximum(first, second), jnp.minimum(first, second)] > 0)

    def wide(ref):
        return jnp.concatenate([ref[m] for m in range(peers)], axis=1)

    def straight(left, right):
        return lax.dot_general(left, right, (((1,), (0,)), ((), ())), preferred_element_type=F32)

    def turned(left, right):
        return lax.dot_general(left, right, (((1,), (1,)), ((), ())), preferred_element_type=F32)

    @pl.when(step == 0)
    def _():
        direct[...] = jnp.zeros_like(direct)

    mirror[...] = jnp.zeros_like(mirror)

    @pl.when(group >= plane)
    def _():
        blocks = []
        for m in range(peers):
            tile = group * peers + m
            use = kept(tile, me)
            mask = use * (
                one(tile > me) * one(row < half) + one(tile == me) * one(row >= col)
            )
            mask = mask.astype(BF16)
            blocks.append(jnp.concatenate([ao[m, 0, p] * mask for p in range(slab)], axis=1))
        direct[...] += straight(wide(coef_group), jnp.concatenate(blocks, axis=0))
        blocks = []
        for m in range(peers):
            tile = plane * peers + m
            use = kept(tile, target) * one(tile < target)
            mask = jnp.full((half, size), use, F32).astype(BF16)
            zero = jnp.zeros((half, size), BF16)
            rows = []
            for p in range(slab):
                rows += [got[0, m, p] * mask, zero]
            blocks.append(jnp.concatenate(rows, axis=0))
        mirror[...] += turned(wide(coef_plane), jnp.concatenate(blocks, axis=1))

    @pl.when(group <= plane)
    def _():
        blocks = []
        for m in range(peers):
            tile = group * peers + m
            use = kept(tile, me)
            mask = use * (
                one(tile < me) * one(row >= half) + one(tile == me) * one(row > col)
            )
            mask = mask.astype(BF16)
            blocks.append(jnp.concatenate([ao[m, 0, p] * mask for p in range(slab)], axis=0))
        direct[...] += turned(wide(coef_group), jnp.concatenate(blocks, axis=1))
        blocks = []
        for m in range(peers):
            tile = plane * peers + m
            use = kept(tile, target) * one(tile > target)
            mask = jnp.full((half, size), use, F32).astype(BF16)
            zero = jnp.zeros((half, size), BF16)
            blocks.append(zero)
            blocks[-1] = jnp.concatenate(
                [jnp.concatenate([zero, got[0, m, p] * mask], axis=0) for p in range(slab)], axis=1
            )
        mirror[...] += straight(wide(coef_plane), jnp.concatenate(blocks, axis=0))

    @pl.when(step == PLANES - 1)
    def _():
        mirror[...] += direct[...]

    chunk = mirror.shape[0] // PLANES
    for z in range(PLANES):
        for p in range(slab):
            out[0, z, p // 2, (p % 2) * chunk : (p % 2 + 1) * chunk, :] = mirror[
                z * chunk : (z + 1) * chunk, p * size : (p + 1) * size
            ]


def partials(ao, got, coefs, block_live, peers):
    _, _, slab, size, _ = ao.shape
    occ = coefs.shape[1]
    me = lax.axis_index("pair")
    place = jnp.stack([me // peers, me]).astype(jnp.int32)

    def at_group(step, place, live):
        return lax.rem(place[0] + 1 + step, PLANES)

    rows = 2 * occ // PLANES
    spec = pltpu.PrefetchScalarGridSpec(
        num_scalar_prefetch=2,
        grid=(PLANES,),
        in_specs=[
            pl.BlockSpec((peers, occ, size), lambda s, p, l: (at_group(s, p, l), 0, 0)),
            pl.BlockSpec((peers, occ, size), lambda s, p, l: (p[0], 0, 0)),
            pl.BlockSpec(
                (peers, 1, slab, size, size), lambda s, p, l: (at_group(s, p, l), 0, 0, 0, 0)
            ),
            pl.BlockSpec(
                (1, peers, slab, size // 2, size), lambda s, p, l: (at_group(s, p, l), 0, 0, 0, 0)
            ),
        ],
        out_specs=pl.BlockSpec(
            (1, PLANES, 2, rows, size), lambda s, p, l: (at_group(s, p, l), 0, 0, 0, 0)
        ),
        scratch_shapes=[pltpu.VMEM((occ, slab * size), F32), pltpu.VMEM((occ, slab * size), F32)],
    )
    return pl.pallas_call(
        functools.partial(partial_kernel, peers),
        grid_spec=spec,
        out_shape=jax.ShapeDtypeStruct((PLANES, PLANES, 2, rows, size), F32),
        compiler_params=pltpu.CompilerParams(vmem_limit_bytes=48 << 20),
    )(place, block_live, coefs, coefs, ao, got)


def ring_kernel(
    peers, ranks, parts, out, own, own_sem, sent, came, send_sem, recv_sem, total, padded, sheet, seen,
    plane_send, plane_recv, line_send, line_recv, line_own,
):
    me, aux = lax.axis_index("pair"), lax.axis_index("aux")
    plane, slot = me // peers, me % peers
    share = parts.shape[3] // (2 * peers)

    def shifted(move):
        return lax.rem(plane + move + PLANES, PLANES)

    def load(group):
        return pltpu.make_async_copy(parts.at[group], own.at[group], own_sem.at[group])

    def hop(way, group, left):
        halves = pl.ds(way, 1) if left == REACH else pl.ds(0, 2)
        return pltpu.make_async_remote_copy(
            src_ref=sent.at[way, group, left - 1, halves],
            dst_ref=came.at[way, group, left - 1, halves],
            send_sem=send_sem.at[way, group, left - 1],
            recv_sem=recv_sem.at[way, group, left - 1],
            device_id=(shifted(1 if way == 0 else -1) * peers + slot, aux),
            device_id_type=MESH,
        )

    def spread(group, step):
        other = lax.rem(slot + step, peers)
        return pltpu.make_async_remote_copy(
            src_ref=sheet.at[group, other],
            dst_ref=seen.at[group, slot],
            send_sem=plane_send.at[group, step],
            recv_sem=plane_recv.at[group, step],
            device_id=(plane * peers + other, aux),
            device_id_type=MESH,
        )

    def line(group, step):
        return pltpu.make_async_remote_copy(
            src_ref=seen.at[group],
            dst_ref=out.at[group, aux],
            send_sem=line_send.at[group, step],
            recv_sem=line_recv.at[group, step],
            device_id=(me, lax.rem(aux + step, ranks)),
            device_id_type=MESH,
        )

    def line_keep(group):
        return pltpu.make_async_copy(seen.at[group], out.at[group, aux], line_own.at[group])

    barrier = pltpu.get_barrier_semaphore()
    for move in (1, -1):
        pl.semaphore_signal(
            barrier, inc=1, device_id=(shifted(move) * peers + slot, aux), device_id_type=MESH
        )
    for step in range(1, peers):
        pl.semaphore_signal(
            barrier,
            inc=1,
            device_id=(plane * peers + lax.rem(slot + step, peers), aux),
            device_id_type=MESH,
        )
    for step in range(1, ranks):
        pl.semaphore_signal(
            barrier, inc=1, device_id=(me, lax.rem(aux + step, ranks)), device_id_type=MESH
        )

    @pl.loop(0, PLANES)
    def _(group):
        load(group).start()

    padded[...] = jnp.zeros_like(padded)
    pl.semaphore_wait(barrier, 2 + peers - 1 + ranks - 1)

    def pass_on(group, left):
        for way in range(2):
            goal = shifted(left if way == 0 else -left)
            if left == REACH:
                sent[way, group, left - 1, way] = own[group, goal, way].astype(BF16)
            else:
                hop(way, group, left + 1).wait_recv()
                for half in range(2):
                    value = own[group, goal, half]
                    if left < REACH - 1 or half == way:
                        value = value + came[way, group, left, half].astype(F32)
                    sent[way, group, left - 1, half] = value.astype(BF16)
            hop(way, group, left).start()

    def finish(group):
        for way in range(2):
            hop(way, group, 1).wait_recv()
        for half in range(2):
            total[half] = (
                own[group, plane, half]
                + came[0, group, 0, half].astype(F32)
                + came[1, group, 0, half].astype(F32)
            )
        for other in range(peers):
            for half in range(2):
                for odd in range(2):
                    start = odd * peers * share + other * share
                    place = (half * 2 + odd) * share
                    padded[other, place : place + share, :] = total[half, start : start + share, :]
            sheet[group, other] = padded[other].astype(BF16)
        seen[group, slot] = sheet[group, slot]
        for step in range(1, peers):
            spread(group, step).start()

    def along(group):
        for step in range(1, peers):
            spread(group, step).wait_recv()
        line_keep(group).start()
        for step in range(1, ranks):
            line(group, step).start()

    @pl.loop(0, PLANES + REACH + 1)
    def _(turn):
        @pl.when(turn < PLANES)
        def _():
            load(turn).wait()
            pass_on(turn, REACH)

        for left in range(REACH - 1, 0, -1):
            group = turn - (REACH - left)

            @pl.when((group >= 0) & (group < PLANES))
            def _(group=group, left=left):
                pass_on(group, left)

        group = turn - REACH

        @pl.when((group >= 0) & (group < PLANES))
        def _(group=group):
            finish(group)

        group = turn - REACH - 1

        @pl.when((group >= 0) & (group < PLANES))
        def _(group=group):
            along(group)

    @pl.loop(0, PLANES)
    def _(group):
        line_keep(group).wait()
        for step in range(1, ranks):
            line(group, step).wait()
        for step in range(1, peers):
            spread(group, step).wait_send()
        for way in range(2):
            for left in range(1, REACH + 1):
                hop(way, group, left).wait_send()


def ring(parts, peers, ranks):
    _, _, _, rows, size = parts.shape
    need = 2 * rows // peers
    room = -(-need // 16) * 16
    return pl.pallas_call(
        functools.partial(ring_kernel, peers, ranks),
        out_shape=jax.ShapeDtypeStruct((PLANES, ranks, peers, room, size), BF16),
        in_specs=[pl.BlockSpec(memory_space=pl.ANY)],
        out_specs=pl.BlockSpec(memory_space=pl.ANY),
        scratch_shapes=[
            pltpu.VMEM(parts.shape, F32),
            pltpu.SemaphoreType.DMA((PLANES,)),
            pltpu.VMEM((2, PLANES, REACH, 2, rows, size), BF16),
            pltpu.VMEM((2, PLANES, REACH, 2, rows, size), BF16),
            pltpu.SemaphoreType.DMA((2, PLANES, REACH)),
            pltpu.SemaphoreType.DMA((2, PLANES, REACH)),
            pltpu.VMEM((2, rows, size), F32),
            pltpu.VMEM((peers, room, size), F32),
            pltpu.VMEM((PLANES, peers, room, size), BF16),
            pltpu.VMEM((PLANES, peers, room, size), BF16),
            pltpu.SemaphoreType.DMA((PLANES, peers)),
            pltpu.SemaphoreType.DMA((PLANES, peers)),
            pltpu.SemaphoreType.DMA((PLANES, ranks)),
            pltpu.SemaphoreType.DMA((PLANES, ranks)),
            pltpu.SemaphoreType.DMA((PLANES,)),
        ],
        compiler_params=pltpu.CompilerParams(
            collective_id=1, has_side_effects=True, vmem_limit_bytes=48 << 20
        ),
        cost_estimate=pl.CostEstimate(flops=0, bytes_accessed=180_000_000, transcendentals=0),
    )(parts)


def fit_kernel(peers, lengths, weights, slabs, out):
    group = pl.program_id(0)
    ranks, _, room, size = slabs.shape[1:]
    panel, share = out.shape[0], out.shape[1]
    inside = lax.broadcasted_iota(jnp.int32, (1, size), 1)
    blocks = [
        jnp.concatenate([slabs[0, r, m] for r in range(ranks)], axis=0) for m in range(peers)
    ]
    result = jnp.dot(
        weights[...], jnp.concatenate(blocks, axis=1), preferred_element_type=F32
    )
    for m in range(peers):
        valid = jnp.broadcast_to(inside < lengths[group * peers + m], (share, size))
        for q in range(panel):
            value = result[16 * q : 16 * q + share, m * size : (m + 1) * size]
            out[q, :, m * size : (m + 1) * size] = jnp.where(valid, value, 0.0).astype(BF16)


def fit(slabs, metric, tile_len, share):
    groups, ranks, peers, room, size = slabs.shape
    slab, panel_all = metric.shape
    panel = panel_all // ranks
    local = lax.dynamic_slice_in_dim(metric, lax.axis_index("aux") * panel, panel, 1)
    weights = jnp.einsum(
        "pq,ij->qipj", local.astype(F32), jnp.eye(16, share, dtype=F32)
    ).reshape(panel * 16, ranks, slab // ranks * share)
    weights = jnp.pad(weights, ((0, 0), (0, 0), (0, room - weights.shape[2])))
    weights = weights.reshape(panel * 16, ranks * room).astype(BF16)
    spec = pltpu.PrefetchScalarGridSpec(
        num_scalar_prefetch=1,
        grid=(groups,),
        in_specs=[
            pl.BlockSpec(weights.shape, lambda g, l: (0, 0)),
            pl.BlockSpec((1, ranks, peers, room, size), lambda g, l: (g, 0, 0, 0, 0)),
        ],
        out_specs=pl.BlockSpec((panel, share, peers * size), lambda g, l: (0, 0, g)),
    )
    return pl.pallas_call(
        functools.partial(fit_kernel, peers),
        grid_spec=spec,
        out_shape=jax.ShapeDtypeStruct((panel, share, groups * peers * size), BF16),
        compiler_params=pltpu.CompilerParams(vmem_limit_bytes=32 << 20),
    )(tile_len, weights, slabs)


def shards(ao_blocks, block_live, tile_len, coeffs, metric_panel):
    pairs, ranks = lax.axis_size("pair"), lax.axis_size("aux")
    peers = pairs // PLANES
    me, aux = lax.axis_index("pair"), lax.axis_index("aux")
    size, occ = coeffs.shape
    inside = jnp.arange(size, dtype=jnp.int32)
    valid = inside < lax.dynamic_index_in_dim(tile_len, me, 0, keepdims=False)
    turned = jnp.where(valid[None, :], jnp.transpose(coeffs), jnp.zeros((), coeffs.dtype))
    part = lax.dynamic_slice_in_dim(turned, aux * (occ // ranks), occ // ranks, 0)
    coefs = lax.all_gather(part[None], ("pair", "aux"), axis=0, tiled=True)
    coefs = coefs.reshape(pairs, occ, size)
    got = exchange(ao_blocks, peers)
    parts = partials(ao_blocks, got, coefs, block_live, peers)
    slabs = ring(parts, peers, ranks)
    return fit(slabs, metric_panel, tile_len, occ // pairs)


def solution(mesh):
    in_specs = (P(None, "pair", "aux", None, None), P(), P(), P("pair", None), P())
    out_specs = P("aux", "pair", None)
    return jax.shard_map(shards, mesh=mesh, in_specs=in_specs, out_specs=out_specs, check_vma=False)
```

```python
import functools

import jax
import jax.numpy as jnp
from jax import lax
from jax.experimental import pallas as pl
from jax.experimental.pallas import tpu as pltpu
from jax.sharding import PartitionSpec as P

MESH = pl.DeviceIdType.MESH
PLANES = 8
REACH = 4
F32 = jnp.float32
BF16 = jnp.bfloat16


def exchange_kernel(
    peers, ranks, ao, mine, got, coefs, send_sem, recv_sem, own_sem, z_send, z_recv, x_send, x_recv,
    y_send, y_recv, core_send, core_recv, mine_sem,
):
    me, aux = lax.axis_index("pair"), lax.axis_index("aux")
    plane, slot = me // peers, me % peers
    chips = peers // 2
    chip, core = slot // 2, slot % 2
    half = ao.shape[3] // 2

    def piece(tile):
        start = pl.multiple_of(jnp.where(tile > me, 0, half), half)
        return ao.at[tile, 0, :, pl.ds(start, half), :]

    def send(group, step):
        other = lax.rem(slot + step, peers)
        return pltpu.make_async_remote_copy(
            src_ref=piece(group * peers + other),
            dst_ref=got.at[group, slot],
            send_sem=send_sem.at[group, step],
            recv_sem=recv_sem.at[group, step],
            device_id=(plane * peers + other, aux),
            device_id_type=MESH,
        )

    def keep(group):
        return pltpu.make_async_copy(
            piece(group * peers + slot), got.at[group, slot], own_sem.at[group]
        )

    def along_z(step):
        return pltpu.make_async_remote_copy(
            src_ref=mine.at[aux],
            dst_ref=coefs.at[plane, slot, aux],
            send_sem=z_send.at[step],
            recv_sem=z_recv.at[step],
            device_id=(lax.rem(plane + step, PLANES) * peers + slot, aux),
            device_id_type=MESH,
        )

    def batch(step, rank):
        source = lax.rem(chip - step + chips, chips) * 2 + core
        return coefs.at[:, source, rank]

    def along_x(step):
        other = lax.rem(chip + step, chips) * 2 + core
        return pltpu.make_async_remote_copy(
            src_ref=batch(0, aux),
            dst_ref=batch(0, aux),
            send_sem=x_send.at[step],
            recv_sem=x_recv.at[step],
            device_id=(plane * peers + other, aux),
            device_id_type=MESH,
        )

    def along_y(step, leg):
        way = 1 if leg == 0 or (leg == 2 and step % 2 == 0) else -1
        rank = aux if leg < 2 else lax.rem(aux - way + ranks, ranks)
        return pltpu.make_async_remote_copy(
            src_ref=batch(step, rank),
            dst_ref=batch(step, rank),
            send_sem=y_send.at[step, leg],
            recv_sem=y_recv.at[step, leg],
            device_id=(me, lax.rem(aux + way + ranks, ranks)),
            device_id_type=MESH,
        )

    def across(step, leg):
        rank = lax.rem(aux + (0, -1, 1, 2)[leg] + ranks, ranks)
        return pltpu.make_async_remote_copy(
            src_ref=batch(step, rank),
            dst_ref=batch(step, rank),
            send_sem=core_send.at[step, leg],
            recv_sem=core_recv.at[step, leg],
            device_id=(me + 1 - 2 * core, aux),
            device_id_type=MESH,
        )

    barrier = pltpu.get_barrier_semaphore()

    def greet(device):
        pl.semaphore_signal(barrier, inc=1, device_id=device, device_id_type=MESH)

    for step in range(1, peers):
        greet((plane * peers + lax.rem(slot + step, peers), aux))
    for step in range(1, PLANES):
        greet((lax.rem(plane + step, PLANES) * peers + slot, aux))
    for step in (1, ranks - 1):
        greet((me, lax.rem(aux + step, ranks)))
    pl.semaphore_wait(barrier, peers + PLANES)

    own_part = pltpu.make_async_copy(mine.at[aux], coefs.at[plane, slot, aux], mine_sem)
    own_part.start()
    for step in range(1, PLANES):
        along_z(step).start()

    def offer(step):
        across(step, 0).start()
        along_y(step, 0).start()
        along_y(step, 1).start()

    def relay(step):
        along_y(step, 0).wait_recv()
        along_y(step, 1).wait_recv()
        along_y(step, 2).start()
        across(step, 1).start()
        across(step, 2).start()

    def close(step):
        along_y(step, 2).wait_recv()
        across(step, 3).start()

    @pl.loop(0, max(PLANES + 1, chips + 4))
    def _(turn):
        @pl.when(turn < PLANES)
        def _():
            keep(turn).start()
            for step in range(1, peers):
                send(turn, step).start()

        @pl.when(turn == 1)
        def _():
            own_part.wait()
            for step in range(1, PLANES):
                along_z(step).wait_recv()
            for step in range(1, chips):
                along_x(step).start()
            offer(0)

        @pl.when(turn == 2)
        def _():
            for step in range(1, chips):
                along_x(step).wait_recv()
                offer(step)

        for step in range(chips):
            @pl.when(turn == 3 + step)
            def _(step=step):
                relay(step)

            @pl.when(turn == 4 + step)
            def _(step=step):
                close(step)

        @pl.when((turn >= 2) & (turn <= PLANES))
        def _():
            for step in range(1, peers):
                send(turn - 2, step).wait_send()

    for step in range(1, peers):
        send(PLANES - 1, step).wait_send()
    for step in range(1, PLANES):
        along_z(step).wait_send()
    for step in range(1, chips):
        along_x(step).wait_send()
    for step in range(chips):
        for leg in range(3):
            along_y(step, leg).wait_send()
        for leg in range(4):
            across(step, leg).wait()

    @pl.loop(0, PLANES)
    def _(group):
        keep(group).wait()
        for step in range(1, peers):
            send(group, step).wait_recv()


def exchange(ao, mine, peers, ranks):
    _, _, slab, size, width = ao.shape
    chips = peers // 2
    dma = pltpu.SemaphoreType.DMA
    return pl.pallas_call(
        functools.partial(exchange_kernel, peers, ranks),
        out_shape=(
            jax.ShapeDtypeStruct((PLANES, peers, slab, size // 2, width), ao.dtype),
            jax.ShapeDtypeStruct((PLANES, peers) + mine.shape, mine.dtype),
        ),
        in_specs=[pl.BlockSpec(memory_space=pl.ANY)] * 2,
        out_specs=(pl.BlockSpec(memory_space=pl.ANY),) * 2,
        scratch_shapes=[
            dma((PLANES, peers)),
            dma((PLANES, peers)),
            dma((PLANES,)),
            dma((PLANES,)),
            dma((PLANES,)),
            dma((chips,)),
            dma((chips,)),
            dma((chips, 3)),
            dma((chips, 3)),
            dma((chips, 4)),
            dma((chips, 4)),
            dma(()),
        ],
        compiler_params=pltpu.CompilerParams(collective_id=0, has_side_effects=True),
    )(ao, mine)


def partial_kernel(peers, place, live, coef_group, coef_plane, ao, got, out, direct, mirror):
    plane, me = place[0], place[1]
    step = pl.program_id(0)
    group = lax.rem(plane + 1 + step, PLANES)
    slab, size = ao.shape[2], ao.shape[3]
    half = size // 2
    target = group * peers + lax.rem(me, peers)
    row = lax.broadcasted_iota(jnp.int32, (size, size), 0)
    col = lax.broadcasted_iota(jnp.int32, (size, size), 1)

    def one(cond):
        return jnp.where(cond, 1.0, 0.0).astype(F32)

    def kept(first, second):
        return one(live[jnp.maximum(first, second), jnp.minimum(first, second)] > 0)

    def wide(ref):
        return jnp.concatenate([ref[m] for m in range(peers)], axis=1)

    def straight(left, right):
        return lax.dot_general(left, right, (((1,), (0,)), ((), ())), preferred_element_type=F32)

    def turned(left, right):
        return lax.dot_general(left, right, (((1,), (1,)), ((), ())), preferred_element_type=F32)

    @pl.when(step == 0)
    def _():
        direct[...] = jnp.zeros_like(direct)

    mirror[...] = jnp.zeros_like(mirror)

    @pl.when(group >= plane)
    def _():
        blocks = []
        for m in range(peers):
            tile = group * peers + m
            use = kept(tile, me)
            mask = use * (
                one(tile > me) * one(row < half) + one(tile == me) * one(row >= col)
            )
            mask = mask.astype(BF16)
            blocks.append(jnp.concatenate([ao[m, 0, p] * mask for p in range(slab)], axis=1))
        direct[...] += straight(wide(coef_group), jnp.concatenate(blocks, axis=0))
        blocks = []
        for m in range(peers):
            tile = plane * peers + m
            use = kept(tile, target) * one(tile < target)
            mask = jnp.full((half, size), use, F32).astype(BF16)
            zero = jnp.zeros((half, size), BF16)
            rows = []
            for p in range(slab):
                rows += [got[0, m, p] * mask, zero]
            blocks.append(jnp.concatenate(rows, axis=0))
        mirror[...] += turned(wide(coef_plane), jnp.concatenate(blocks, axis=1))

    @pl.when(group <= plane)
    def _():
        blocks = []
        for m in range(peers):
            tile = group * peers + m
            use = kept(tile, me)
            mask = use * (
                one(tile < me) * one(row >= half) + one(tile == me) * one(row > col)
            )
            mask = mask.astype(BF16)
            blocks.append(jnp.concatenate([ao[m, 0, p] * mask for p in range(slab)], axis=0))
        direct[...] += turned(wide(coef_group), jnp.concatenate(blocks, axis=1))
        blocks = []
        for m in range(peers):
            tile = plane * peers + m
            use = kept(tile, target) * one(tile > target)
            mask = jnp.full((half, size), use, F32).astype(BF16)
            zero = jnp.zeros((half, size), BF16)
            blocks.append(zero)
            blocks[-1] = jnp.concatenate(
                [jnp.concatenate([zero, got[0, m, p] * mask], axis=0) for p in range(slab)], axis=1
            )
        mirror[...] += straight(wide(coef_plane), jnp.concatenate(blocks, axis=0))

    @pl.when(step == PLANES - 1)
    def _():
        mirror[...] += direct[...]

    chunk = mirror.shape[0] // PLANES
    for z in range(PLANES):
        for p in range(slab):
            out[0, z, p // 2, (p % 2) * chunk : (p % 2 + 1) * chunk, :] = mirror[
                z * chunk : (z + 1) * chunk, p * size : (p + 1) * size
            ]


def partials(ao, got, coefs, block_live, peers):
    _, _, slab, size, _ = ao.shape
    occ = coefs.shape[1]
    me = lax.axis_index("pair")
    place = jnp.stack([me // peers, me]).astype(jnp.int32)

    def at_group(step, place, live):
        return lax.rem(place[0] + 1 + step, PLANES)

    rows = 2 * occ // PLANES
    spec = pltpu.PrefetchScalarGridSpec(
        num_scalar_prefetch=2,
        grid=(PLANES,),
        in_specs=[
            pl.BlockSpec((peers, occ, size), lambda s, p, l: (at_group(s, p, l), 0, 0)),
            pl.BlockSpec((peers, occ, size), lambda s, p, l: (p[0], 0, 0)),
            pl.BlockSpec(
                (peers, 1, slab, size, size), lambda s, p, l: (at_group(s, p, l), 0, 0, 0, 0)
            ),
            pl.BlockSpec(
                (1, peers, slab, size // 2, size), lambda s, p, l: (at_group(s, p, l), 0, 0, 0, 0)
            ),
        ],
        out_specs=pl.BlockSpec(
            (1, PLANES, 2, rows, size), lambda s, p, l: (at_group(s, p, l), 0, 0, 0, 0)
        ),
        scratch_shapes=[pltpu.VMEM((occ, slab * size), F32), pltpu.VMEM((occ, slab * size), F32)],
    )
    return pl.pallas_call(
        functools.partial(partial_kernel, peers),
        grid_spec=spec,
        out_shape=jax.ShapeDtypeStruct((PLANES, PLANES, 2, rows, size), F32),
        compiler_params=pltpu.CompilerParams(vmem_limit_bytes=48 << 20),
    )(place, block_live, coefs, coefs, ao, got)


def ring_kernel(
    peers, ranks, parts, out, own, own_sem, sent, came, send_sem, recv_sem, total, padded, sheet, seen,
    plane_send, plane_recv, line_send, line_recv, line_own,
):
    me, aux = lax.axis_index("pair"), lax.axis_index("aux")
    plane, slot = me // peers, me % peers
    share = parts.shape[3] // (2 * peers)

    def shifted(move):
        return lax.rem(plane + move + PLANES, PLANES)

    def load(group):
        return pltpu.make_async_copy(parts.at[group], own.at[group], own_sem.at[group])

    def hop(way, group, left):
        halves = pl.ds(way, 1) if left == REACH else pl.ds(0, 2)
        return pltpu.make_async_remote_copy(
            src_ref=sent.at[way, group, left - 1, halves],
            dst_ref=came.at[way, group, left - 1, halves],
            send_sem=send_sem.at[way, group, left - 1],
            recv_sem=recv_sem.at[way, group, left - 1],
            device_id=(shifted(1 if way == 0 else -1) * peers + slot, aux),
            device_id_type=MESH,
        )

    def spread(group, step):
        other = lax.rem(slot + step, peers)
        return pltpu.make_async_remote_copy(
            src_ref=sheet.at[group, other],
            dst_ref=seen.at[group, slot],
            send_sem=plane_send.at[group, step],
            recv_sem=plane_recv.at[group, step],
            device_id=(plane * peers + other, aux),
            device_id_type=MESH,
        )

    def line(group, step):
        return pltpu.make_async_remote_copy(
            src_ref=seen.at[group],
            dst_ref=out.at[group, aux],
            send_sem=line_send.at[group, step],
            recv_sem=line_recv.at[group, step],
            device_id=(me, lax.rem(aux + step, ranks)),
            device_id_type=MESH,
        )

    def line_keep(group):
        return pltpu.make_async_copy(seen.at[group], out.at[group, aux], line_own.at[group])

    barrier = pltpu.get_barrier_semaphore()
    for move in (1, -1):
        pl.semaphore_signal(
            barrier, inc=1, device_id=(shifted(move) * peers + slot, aux), device_id_type=MESH
        )
    for step in range(1, peers):
        pl.semaphore_signal(
            barrier,
            inc=1,
            device_id=(plane * peers + lax.rem(slot + step, peers), aux),
            device_id_type=MESH,
        )
    for step in range(1, ranks):
        pl.semaphore_signal(
            barrier, inc=1, device_id=(me, lax.rem(aux + step, ranks)), device_id_type=MESH
        )

    @pl.loop(0, PLANES)
    def _(group):
        load(group).start()

    padded[...] = jnp.zeros_like(padded)
    pl.semaphore_wait(barrier, 2 + peers - 1 + ranks - 1)

    def pass_on(group, left):
        for way in range(2):
            goal = shifted(left if way == 0 else -left)
            if left == REACH:
                sent[way, group, left - 1, way] = own[group, goal, way].astype(BF16)
            else:
                hop(way, group, left + 1).wait_recv()
                for half in range(2):
                    value = own[group, goal, half]
                    if left < REACH - 1 or half == way:
                        value = value + came[way, group, left, half].astype(F32)
                    sent[way, group, left - 1, half] = value.astype(BF16)
            hop(way, group, left).start()

    def finish(group):
        for way in range(2):
            hop(way, group, 1).wait_recv()
        for half in range(2):
            total[half] = (
                own[group, plane, half]
                + came[0, group, 0, half].astype(F32)
                + came[1, group, 0, half].astype(F32)
            )
        for other in range(peers):
            for half in range(2):
                for odd in range(2):
                    start = odd * peers * share + other * share
                    place = (half * 2 + odd) * share
                    padded[other, place : place + share, :] = total[half, start : start + share, :]
            sheet[group, other] = padded[other].astype(BF16)
        seen[group, slot] = sheet[group, slot]
        for step in range(1, peers):
            spread(group, step).start()

    def along(group):
        for step in range(1, peers):
            spread(group, step).wait_recv()
        line_keep(group).start()
        for step in range(1, ranks):
            line(group, step).start()

    @pl.loop(0, PLANES + REACH + 1)
    def _(turn):
        @pl.when(turn < PLANES)
        def _():
            load(turn).wait()
            pass_on(turn, REACH)

        for left in range(REACH - 1, 0, -1):
            group = turn - (REACH - left)

            @pl.when((group >= 0) & (group < PLANES))
            def _(group=group, left=left):
                pass_on(group, left)

        group = turn - REACH

        @pl.when((group >= 0) & (group < PLANES))
        def _(group=group):
            finish(group)

        group = turn - REACH - 1

        @pl.when((group >= 0) & (group < PLANES))
        def _(group=group):
            along(group)

    @pl.loop(0, PLANES)
    def _(group):
        line_keep(group).wait()
        for step in range(1, ranks):
            line(group, step).wait()
        for step in range(1, peers):
            spread(group, step).wait_send()
        for way in range(2):
            for left in range(1, REACH + 1):
                hop(way, group, left).wait_send()


def ring(parts, peers, ranks):
    _, _, _, rows, size = parts.shape
    need = 2 * rows // peers
    room = -(-need // 16) * 16
    return pl.pallas_call(
        functools.partial(ring_kernel, peers, ranks),
        out_shape=jax.ShapeDtypeStruct((PLANES, ranks, peers, room, size), BF16),
        in_specs=[pl.BlockSpec(memory_space=pl.ANY)],
        out_specs=pl.BlockSpec(memory_space=pl.ANY),
        scratch_shapes=[
            pltpu.VMEM(parts.shape, F32),
            pltpu.SemaphoreType.DMA((PLANES,)),
            pltpu.VMEM((2, PLANES, REACH, 2, rows, size), BF16),
            pltpu.VMEM((2, PLANES, REACH, 2, rows, size), BF16),
            pltpu.SemaphoreType.DMA((2, PLANES, REACH)),
            pltpu.SemaphoreType.DMA((2, PLANES, REACH)),
            pltpu.VMEM((2, rows, size), F32),
            pltpu.VMEM((peers, room, size), F32),
            pltpu.VMEM((PLANES, peers, room, size), BF16),
            pltpu.VMEM((PLANES, peers, room, size), BF16),
            pltpu.SemaphoreType.DMA((PLANES, peers)),
            pltpu.SemaphoreType.DMA((PLANES, peers)),
            pltpu.SemaphoreType.DMA((PLANES, ranks)),
            pltpu.SemaphoreType.DMA((PLANES, ranks)),
            pltpu.SemaphoreType.DMA((PLANES,)),
        ],
        compiler_params=pltpu.CompilerParams(
            collective_id=1, has_side_effects=True, vmem_limit_bytes=48 << 20
        ),
        cost_estimate=pl.CostEstimate(flops=0, bytes_accessed=180_000_000, transcendentals=0),
    )(parts)


def fit_kernel(peers, lengths, weights, slabs, out):
    group = pl.program_id(0)
    ranks, _, room, size = slabs.shape[1:]
    panel, share = out.shape[0], out.shape[1]
    inside = lax.broadcasted_iota(jnp.int32, (1, size), 1)
    blocks = [
        jnp.concatenate([slabs[0, r, m] for r in range(ranks)], axis=0) for m in range(peers)
    ]
    result = jnp.dot(
        weights[...], jnp.concatenate(blocks, axis=1), preferred_element_type=F32
    )
    for m in range(peers):
        valid = jnp.broadcast_to(inside < lengths[group * peers + m], (share, size))
        for q in range(panel):
            value = result[16 * q : 16 * q + share, m * size : (m + 1) * size]
            out[q, :, m * size : (m + 1) * size] = jnp.where(valid, value, 0.0).astype(BF16)


def fit(slabs, metric, tile_len, share):
    groups, ranks, peers, room, size = slabs.shape
    slab, panel_all = metric.shape
    panel = panel_all // ranks
    local = lax.dynamic_slice_in_dim(metric, lax.axis_index("aux") * panel, panel, 1)
    weights = jnp.einsum(
        "pq,ij->qipj", local.astype(F32), jnp.eye(16, share, dtype=F32)
    ).reshape(panel * 16, ranks, slab // ranks * share)
    weights = jnp.pad(weights, ((0, 0), (0, 0), (0, room - weights.shape[2])))
    weights = weights.reshape(panel * 16, ranks * room).astype(BF16)
    spec = pltpu.PrefetchScalarGridSpec(
        num_scalar_prefetch=1,
        grid=(groups,),
        in_specs=[
            pl.BlockSpec(weights.shape, lambda g, l: (0, 0)),
            pl.BlockSpec((1, ranks, peers, room, size), lambda g, l: (g, 0, 0, 0, 0)),
        ],
        out_specs=pl.BlockSpec((panel, share, peers * size), lambda g, l: (0, 0, g)),
    )
    return pl.pallas_call(
        functools.partial(fit_kernel, peers),
        grid_spec=spec,
        out_shape=jax.ShapeDtypeStruct((panel, share, groups * peers * size), BF16),
        compiler_params=pltpu.CompilerParams(vmem_limit_bytes=32 << 20),
    )(tile_len, weights, slabs)


def shards(ao_blocks, block_live, tile_len, coeffs, metric_panel):
    pairs, ranks = lax.axis_size("pair"), lax.axis_size("aux")
    peers = pairs // PLANES
    me = lax.axis_index("pair")
    size, occ = coeffs.shape
    inside = jnp.arange(size, dtype=jnp.int32)
    valid = inside < lax.dynamic_index_in_dim(tile_len, me, 0, keepdims=False)
    turned = jnp.where(valid[None, :], jnp.transpose(coeffs), jnp.zeros((), coeffs.dtype))
    mine = turned.reshape(ranks, occ // ranks, size)
    got, coefs = exchange(ao_blocks, mine, peers, ranks)
    coefs = coefs.reshape(pairs, occ, size)
    parts = partials(ao_blocks, got, coefs, block_live, peers)
    slabs = ring(parts, peers, ranks)
    return fit(slabs, metric_panel, tile_len, occ // pairs)


def solution(mesh):
    in_specs = (P(None, "pair", "aux", None, None), P(), P(), P("pair", None), P())
    out_specs = P("aux", "pair", None)
    return jax.shard_map(shards, mesh=mesh, in_specs=in_specs, out_specs=out_specs, check_vma=False)
```

```python
import functools

import jax
import jax.numpy as jnp
from jax import lax
from jax.experimental import pallas as pl
from jax.experimental.pallas import tpu as pltpu
from jax.sharding import PartitionSpec as P

MESH = pl.DeviceIdType.MESH
PLANES = 8
REACH = 4
F32 = jnp.float32
BF16 = jnp.bfloat16


def half_kernel(
    peers, ranks, live, lengths, coeffs, ao, out,
    mine, coefs, got, held, diagonal, wide_own, high_own, direct, mirror, own, sent, came,
    total, padded, sheet, seen,
    x_send, x_recv, x_own, held_sem, mine_sem, gz_send, gz_recv, gx_send, gx_recv, gy_send, gy_recv,
    gc_send, gc_recv, bx_send, bx_recv, bz_send, bz_recv, bc_send, bc_recv,
    send_sem, recv_sem, plane_send, plane_recv, line_send, line_recv, line_own,
):
    me, aux = lax.axis_index("pair"), lax.axis_index("aux")
    plane, slot = me // peers, me % peers
    chips = peers // 2
    chip, core = slot // 2, slot % 2
    slab, half, size = got.shape[2:]
    occ = mine.shape[0]
    low_rows = quarter_rows(occ, ranks)
    rest = pl.ds(low_rows * ranks, occ - low_rows * ranks)
    chunk = occ // PLANES
    share = chunk // peers
    begin = PLANES - 2

    def remote(src, dst, sends, recvs, device):
        return pltpu.make_async_remote_copy(
            src_ref=src, dst_ref=dst, send_sem=sends, recv_sem=recvs,
            device_id=device, device_id_type=MESH,
        )

    def shifted(move):
        return lax.rem(plane + move + PLANES, PLANES)

    def in_plane(step):
        return lax.rem(slot + step, peers)

    def in_line(step):
        return lax.rem(aux + step + ranks, ranks)

    def in_row(step):
        return lax.rem(chip + step + chips, chips)

    def quarter(rank):
        return pl.ds(pl.multiple_of(rank * low_rows, 16), low_rows)

    def gather_z(step):
        return remote(
            mine.at[quarter(aux)], coefs.at[plane, core, chip, quarter(aux)],
            gz_send.at[step], gz_recv.at[step], (shifted(step) * peers + slot, aux),
        )

    def batch(step, rank):
        return coefs.at[:, core, in_row(-step), quarter(rank)]

    def gather_x(step):
        return remote(
            batch(0, aux), batch(0, aux), gx_send.at[step], gx_recv.at[step],
            (plane * peers + in_row(step) * 2 + core, aux),
        )

    def gather_y(step, leg):
        way = 1 if leg == 0 or (leg == 2 and step % 2 == 0) else -1
        rank = aux if leg < 2 else in_line(-way)
        return remote(
            batch(step, rank), batch(step, rank), gy_send.at[step, leg], gy_recv.at[step, leg],
            (me, in_line(way)),
        )

    other_core = (me + 1 - 2 * core, aux)

    def gather_core(step, leg):
        rank = in_line((0, -1, 1, 2)[leg])
        return remote(
            batch(step, rank), batch(step, rank), gc_send.at[step, leg], gc_recv.at[step, leg],
            other_core,
        )

    def rest_x(step):
        return remote(
            mine.at[rest], coefs.at[plane, core, chip, rest], bx_send.at[step], bx_recv.at[step],
            (plane * peers + in_row(step) * 2 + core, aux),
        )

    def rest_z(way, count):
        sign = 1 if way == 0 else -1
        middle = max(chips // 2, 1)
        chunk_chips = pl.ds(0, chips)
        if count == REACH:
            chunk_chips = pl.ds(0, middle) if way == 0 else pl.ds(chips - middle, middle)
        part = coefs.at[shifted(-sign * (count - 1)), core, chunk_chips, rest]
        return remote(
            part, part, bz_send.at[way, count - 1], bz_recv.at[way, count - 1],
            (shifted(sign) * peers + slot, aux),
        )

    def rest_core(move):
        part = coefs.at[shifted(move), core, :, rest]
        return remote(
            part, part, bc_send.at[move + REACH - 1], bc_recv.at[move + REACH - 1], other_core
        )

    own_quarter = pltpu.make_async_copy(
        mine.at[quarter(aux)], coefs.at[plane, core, chip, quarter(aux)], mine_sem.at[0]
    )
    own_rest = pltpu.make_async_copy(
        mine.at[rest], coefs.at[plane, core, chip, rest], mine_sem.at[1]
    )

    def piece(tile):
        start = pl.multiple_of(jnp.where(tile > me, 0, half), half)
        return ao.at[tile, 0, :, pl.ds(start, half), :]

    def send(group, step):
        other = in_plane(step)
        return remote(
            piece(group * peers + other), got.at[group, slot],
            x_send.at[group, step], x_recv.at[group, step], (plane * peers + other, aux),
        )

    def keep(group):
        return pltpu.make_async_copy(
            piece(group * peers + slot), got.at[group, slot], x_own.at[group]
        )

    def hold(group, m):
        return pltpu.make_async_copy(
            piece(group * peers + m), held.at[group, m], held_sem.at[group, m]
        )

    hold_diagonal = pltpu.make_async_copy(ao.at[me, 0], diagonal, mine_sem.at[2])

    def hop(way, group, left):
        halves = pl.ds(way, 1) if left == REACH else pl.ds(0, 2)
        return remote(
            sent.at[way, group, left - 1, halves], came.at[way, group, left - 1, halves],
            send_sem.at[way, group, left - 1], recv_sem.at[way, group, left - 1],
            (shifted(1 if way == 0 else -1) * peers + slot, aux),
        )

    def spread(group, step):
        other = in_plane(step)
        return remote(
            sheet.at[group, other], seen.at[group, slot],
            plane_send.at[group, step], plane_recv.at[group, step], (plane * peers + other, aux),
        )

    def line(group, step):
        return remote(
            seen.at[group], out.at[group, aux], line_send.at[group, step], line_recv.at[group, step],
            (me, in_line(step)),
        )

    def line_keep(group):
        return pltpu.make_async_copy(seen.at[group], out.at[group, aux], line_own.at[group])

    barrier = pltpu.get_barrier_semaphore()

    def greet(device):
        pl.semaphore_signal(barrier, inc=1, device_id=device, device_id_type=MESH)

    for step in range(1, peers):
        greet((plane * peers + in_plane(step), aux))
    for step in range(1, PLANES):
        greet((shifted(step) * peers + slot, aux))
    for step in range(1, ranks):
        greet((me, in_line(step)))

    hold_diagonal.start()

    @pl.loop(0, PLANES)
    def _(group):
        for m in range(peers):
            hold(group, m).start()

    column = lax.broadcasted_iota(jnp.int32, (occ, size), 1)
    valid = jnp.where(column < lengths[me], 1.0, 0.0).astype(F32)
    mine[...] = (jnp.transpose(coeffs[...].astype(F32)) * valid).astype(BF16)
    padded[...] = jnp.zeros_like(padded)
    pl.semaphore_wait(barrier, peers - 1 + PLANES - 1 + ranks - 1)

    own_quarter.start()
    own_rest.start()
    for step in range(1, chips):
        rest_x(step).start()
    for step in range(1, PLANES):
        gather_z(step).start()

    def offer(step):
        gather_y(step, 0).start()
        gather_y(step, 1).start()
        gather_core(step, 0).start()

    def relay(step):
        gather_y(step, 0).wait_recv()
        gather_y(step, 1).wait_recv()
        gather_y(step, 2).start()
        gather_core(step, 1).start()
        gather_core(step, 2).start()

    def close(step):
        gather_y(step, 2).wait_recv()
        gather_core(step, 3).start()

    def rest_next(count):
        for way in range(2):
            rest_z(way, count).wait_recv()
        for way in range(2):
            if count < REACH:
                rest_z(way, count + 1).start()
        if count < REACH:
            rest_core(-count).start()
            rest_core(count).start()
        else:
            rest_core(REACH).start()

    def gather_turn(turn):
        @pl.when(turn == 1)
        def _():
            own_quarter.wait()
            own_rest.wait()
            for step in range(1, PLANES):
                gather_z(step).wait_recv()
            for step in range(1, chips):
                gather_x(step).start()
            offer(0)
            for step in range(1, chips):
                rest_x(step).wait_recv()
            rest_z(0, 1).start()
            rest_z(1, 1).start()
            rest_core(0).start()

        @pl.when(turn == 2)
        def _():
            for step in range(1, chips):
                gather_x(step).wait_recv()
                offer(step)
            rest_next(1)

        @pl.when(turn == 3)
        def _():
            for step in range(chips // 2):
                relay(step)
            rest_next(2)

        @pl.when(turn == 4)
        def _():
            for step in range(chips // 2):
                close(step)
            for step in range(chips // 2, chips):
                relay(step)
            rest_next(3)

        @pl.when(turn == 5)
        def _():
            for step in range(chips // 2, chips):
                close(step)
            rest_next(REACH)
            for step in range(chips):
                for leg in range(4):
                    gather_core(step, leg).wait_recv()
            for move in range(1 - REACH, REACH + 1):
                rest_core(move).wait_recv()

    def one(cond):
        return jnp.where(cond, 1.0, 0.0).astype(F32)

    def kept(first, second):
        return one(live[jnp.maximum(first, second), jnp.minimum(first, second)] > 0)

    def coef(group, m):
        return coefs[group, m % 2, m // 2]

    def wide(group):
        return jnp.concatenate([coef(group, m) for m in range(peers)], axis=1)

    def cut(group, start):
        return jnp.concatenate(
            [coef(group, m)[:, start : start + half] for m in range(peers)], axis=1
        )

    def straight(left, right):
        return lax.dot_general(left, right, (((1,), (0,)), ((), ())), preferred_element_type=F32)

    def turned(left, right):
        return lax.dot_general(left, right, (((1,), (1,)), ((), ())), preferred_element_type=F32)

    def scaled(block, factor):
        return block * jnp.full((half, size), factor, F32).astype(BF16)

    lower = lax.broadcasted_iota(jnp.int32, (occ, size), 1) < half

    def place(acc, result, upper):
        for p in range(slab):
            value = result[:, (p // 2) * size : (p // 2 + 1) * size]
            if (p % 2 == 0) == upper:
                value = pltpu.roll(value, half, 1)
            value = jnp.where(lower, 0.0, value) if upper else jnp.where(lower, value, 0.0)
            acc[:, p * size : (p + 1) * size] += value

    def stacked(source, group, factors):
        return jnp.concatenate(
            [
                jnp.concatenate([scaled(source[group, m, p], factors[m]) for p in range(slab)], axis=1)
                for m in range(peers)
            ],
            axis=0,
        )

    def beside(source, group, factors):
        return jnp.concatenate(
            [
                jnp.concatenate([scaled(source[group, m, p], factors[m]) for p in range(slab)], axis=0)
                for m in range(peers)
            ],
            axis=1,
        )

    def sum_direct():
        hold_diagonal.wait()
        row = lax.broadcasted_iota(jnp.int32, (size, size), 0)
        col = lax.broadcasted_iota(jnp.int32, (size, size), 1)
        factor = kept(me, me)
        tril = (factor * one(row >= col)).astype(BF16)
        strict = (factor * one(row > col)).astype(BF16)
        blocks = [diagonal[p] * tril for p in range(slab)]
        direct[...] = straight(mine[...], jnp.concatenate(blocks, axis=1))
        blocks = [diagonal[p] * strict for p in range(slab)]
        direct[...] += turned(mine[...], jnp.concatenate(blocks, axis=0))

        @pl.loop(0, PLANES)
        def _(group):
            for m in range(peers):
                hold(group, m).wait()

            @pl.when(group >= plane)
            def _():
                tiles = [group * peers + m for m in range(peers)]
                factors = [kept(tile, me) * one(tile > me) for tile in tiles]
                direct[...] += straight(cut(group, 0), stacked(held, group, factors))

            @pl.when(group <= plane)
            def _():
                tiles = [group * peers + m for m in range(peers)]
                factors = [kept(tile, me) * one(tile < me) for tile in tiles]
                place(direct, turned(wide(group), beside(held, group, factors)), True)

    def sum_mirror(group):
        keep(group).wait()
        for step in range(1, peers):
            send(group, step).wait_recv()
        target = group * peers + slot
        tiles = [plane * peers + m for m in range(peers)]

        @pl.when(group == plane)
        def _():
            mirror[...] = direct[...]

        @pl.when(group != plane)
        def _():
            mirror[...] = jnp.zeros_like(mirror)

        @pl.when(group >= plane)
        def _():
            factors = [kept(tile, target) * one(tile < target) for tile in tiles]
            place(mirror, turned(wide_own[...], beside(got, group, factors)), False)

        @pl.when(group <= plane)
        def _():
            factors = [kept(tile, target) * one(tile > target) for tile in tiles]
            mirror[...] += straight(high_own[...], stacked(got, group, factors))

        for z in range(PLANES):
            for p in range(slab):
                own[group, z, p // 2, (p % 2) * chunk : (p % 2 + 1) * chunk, :] = mirror[
                    z * chunk : (z + 1) * chunk, p * size : (p + 1) * size
                ]

    def pass_on(group, left):
        for way in range(2):
            goal = shifted(left if way == 0 else -left)
            if left == REACH:
                sent[way, group, left - 1, way] = own[group, goal, way].astype(BF16)
            else:
                hop(way, group, left + 1).wait_recv()
                for part in range(2):
                    value = own[group, goal, part]
                    if left < REACH - 1 or part == way:
                        value = value + came[way, group, left, part].astype(F32)
                    sent[way, group, left - 1, part] = value.astype(BF16)
            hop(way, group, left).start()

    def finish(group):
        for way in range(2):
            hop(way, group, 1).wait_recv()
        for part in range(2):
            total[part] = (
                own[group, plane, part]
                + came[0, group, 0, part].astype(F32)
                + came[1, group, 0, part].astype(F32)
            )
        for other in range(peers):
            for part in range(2):
                for odd in range(2):
                    start = odd * chunk + other * share
                    spot = (part * 2 + odd) * share
                    padded[other, spot : spot + share, :] = total[part, start : start + share, :]
            sheet[group, other] = padded[other].astype(BF16)
        seen[group, slot] = sheet[group, slot]
        for step in range(1, peers):
            spread(group, step).start()

    def along(group):
        for step in range(1, peers):
            spread(group, step).wait_recv()
        line_keep(group).start()
        for step in range(1, ranks):
            line(group, step).start()

    @pl.loop(0, begin + PLANES + REACH + 1)
    def _(turn):
        for left in range(1, REACH):
            group = turn - begin - (REACH - left)

            @pl.when((group >= 0) & (group < PLANES))
            def _(group=group, left=left):
                pass_on(group, left)

        gather_turn(turn)

        @pl.when(turn < PLANES)
        def _():
            keep(turn).start()
            for step in range(1, peers):
                send(turn, step).start()

        group = turn - begin - REACH

        @pl.when((group >= 0) & (group < PLANES))
        def _(group=group):
            finish(group)

        group = turn - begin - REACH - 1

        @pl.when((group >= 0) & (group < PLANES))
        def _(group=group):
            along(group)

        @pl.when(turn == begin)
        def _():
            wide_own[...] = wide(plane)
            high_own[...] = cut(plane, half)
            sum_direct()

        group = turn - begin

        @pl.when((group >= 0) & (group < PLANES))
        def _(group=group):
            sum_mirror(group)
            pass_on(group, REACH)

        @pl.when((turn >= 2) & (turn < PLANES + 2))
        def _():
            for step in range(1, peers):
                send(turn - 2, step).wait_send()

    for step in range(1, PLANES):
        gather_z(step).wait_send()
    for step in range(1, chips):
        gather_x(step).wait_send()
        rest_x(step).wait_send()
    for step in range(chips):
        for leg in range(3):
            gather_y(step, leg).wait_send()
        for leg in range(4):
            gather_core(step, leg).wait_send()
    for move in range(1 - REACH, REACH + 1):
        rest_core(move).wait_send()
    for way in range(2):
        for count in range(1, REACH + 1):
            rest_z(way, count).wait_send()

    @pl.loop(0, PLANES)
    def _(group):
        line_keep(group).wait()
        for step in range(1, ranks):
            line(group, step).wait()
        for step in range(1, peers):
            spread(group, step).wait_send()
        for way in range(2):
            for left in range(1, REACH + 1):
                hop(way, group, left).wait_send()


def quarter_rows(occ, ranks):
    return 16 * max(1, (occ * 5 // 9) // (16 * ranks))


def half_sums(ao, block_live, tile_len, coeffs, peers, ranks):
    _, _, slab, size, _ = ao.shape
    occ = coeffs.shape[1]
    chips = peers // 2
    rows = 2 * occ // PLANES
    room = -(-(2 * rows // peers) // 16) * 16
    dma = pltpu.SemaphoreType.DMA
    pieces = (PLANES, peers, slab, size // 2, size)
    hops = (2, PLANES, REACH)
    return pl.pallas_call(
        functools.partial(half_kernel, peers, ranks),
        out_shape=jax.ShapeDtypeStruct((PLANES, ranks, peers, room, size), BF16),
        in_specs=[
            pl.BlockSpec(memory_space=pltpu.SMEM),
            pl.BlockSpec(memory_space=pltpu.SMEM),
            pl.BlockSpec(memory_space=pltpu.VMEM),
            pl.BlockSpec(memory_space=pl.ANY),
        ],
        out_specs=pl.BlockSpec(memory_space=pl.ANY),
        scratch_shapes=[
            pltpu.VMEM((occ, size), BF16),
            pltpu.VMEM((PLANES, 2, chips, occ, size), BF16),
            pltpu.VMEM(pieces, BF16),
            pltpu.VMEM(pieces, BF16),
            pltpu.VMEM((slab, size, size), BF16),
            pltpu.VMEM((occ, peers * size), BF16),
            pltpu.VMEM((occ, peers * size // 2), BF16),
            pltpu.VMEM((occ, slab * size), F32),
            pltpu.VMEM((occ, slab * size), F32),
            pltpu.VMEM((PLANES, PLANES, 2, rows, size), F32),
            pltpu.VMEM(hops + (2, rows, size), BF16),
            pltpu.VMEM(hops + (2, rows, size), BF16),
            pltpu.VMEM((2, rows, size), F32),
            pltpu.VMEM((peers, room, size), F32),
            pltpu.VMEM((PLANES, peers, room, size), BF16),
            pltpu.VMEM((PLANES, peers, room, size), BF16),
            dma((PLANES, peers)), dma((PLANES, peers)), dma((PLANES,)), dma((PLANES, peers)), dma((3,)),
            dma((PLANES,)), dma((PLANES,)), dma((chips,)), dma((chips,)),
            dma((chips, 3)), dma((chips, 3)), dma((chips, 4)), dma((chips, 4)),
            dma((chips,)), dma((chips,)), dma((2, REACH)), dma((2, REACH)),
            dma((2 * REACH,)), dma((2 * REACH,)),
            dma(hops), dma(hops), dma((PLANES, peers)), dma((PLANES, peers)),
            dma((PLANES, ranks)), dma((PLANES, ranks)), dma((PLANES,)),
        ],
        compiler_params=pltpu.CompilerParams(
            collective_id=0, has_side_effects=True, vmem_limit_bytes=60 << 20
        ),
    )(block_live, tile_len, coeffs, ao)


def fit_kernel(peers, lengths, weights, slabs, out):
    group = pl.program_id(0)
    ranks, _, room, size = slabs.shape[1:]
    panel, share = out.shape[0], out.shape[1]
    inside = lax.broadcasted_iota(jnp.int32, (1, size), 1)
    blocks = [
        jnp.concatenate([slabs[0, r, m] for r in range(ranks)], axis=0) for m in range(peers)
    ]
    result = jnp.dot(
        weights[...], jnp.concatenate(blocks, axis=1), preferred_element_type=F32
    )
    for m in range(peers):
        valid = jnp.broadcast_to(inside < lengths[group * peers + m], (share, size))
        for q in range(panel):
            value = result[16 * q : 16 * q + share, m * size : (m + 1) * size]
            out[q, :, m * size : (m + 1) * size] = jnp.where(valid, value, 0.0).astype(BF16)


def fit(slabs, metric, tile_len, share):
    groups, ranks, peers, room, size = slabs.shape
    slab, panel_all = metric.shape
    panel = panel_all // ranks
    local = lax.dynamic_slice_in_dim(metric, lax.axis_index("aux") * panel, panel, 1)
    weights = jnp.einsum(
        "pq,ij->qipj", local.astype(F32), jnp.eye(16, share, dtype=F32)
    ).reshape(panel * 16, ranks, slab // ranks * share)
    weights = jnp.pad(weights, ((0, 0), (0, 0), (0, room - weights.shape[2])))
    weights = weights.reshape(panel * 16, ranks * room).astype(BF16)
    spec = pltpu.PrefetchScalarGridSpec(
        num_scalar_prefetch=1,
        grid=(groups,),
        in_specs=[
            pl.BlockSpec(weights.shape, lambda g, l: (0, 0)),
            pl.BlockSpec((1, ranks, peers, room, size), lambda g, l: (g, 0, 0, 0, 0)),
        ],
        out_specs=pl.BlockSpec((panel, share, peers * size), lambda g, l: (0, 0, g)),
    )
    return pl.pallas_call(
        functools.partial(fit_kernel, peers),
        grid_spec=spec,
        out_shape=jax.ShapeDtypeStruct((panel, share, groups * peers * size), BF16),
        compiler_params=pltpu.CompilerParams(vmem_limit_bytes=32 << 20),
    )(tile_len, weights, slabs)


def shards(ao_blocks, block_live, tile_len, coeffs, metric_panel):
    pairs, ranks = lax.axis_size("pair"), lax.axis_size("aux")
    peers = pairs // PLANES
    occ = coeffs.shape[1]
    slabs = half_sums(ao_blocks, block_live, tile_len, coeffs, peers, ranks)
    return fit(slabs, metric_panel, tile_len, occ // pairs)


def solution(mesh):
    in_specs = (P(None, "pair", "aux", None, None), P(), P(), P("pair", None), P())
    out_specs = P("aux", "pair", None)
    return jax.shard_map(shards, mesh=mesh, in_specs=in_specs, out_specs=out_specs, check_vma=False)
```

```python
import functools

import jax
import jax.numpy as jnp
from jax import lax
from jax.experimental import pallas as pl
from jax.experimental.pallas import tpu as pltpu
from jax.sharding import PartitionSpec as P

MESH = pl.DeviceIdType.MESH
PLANES = 8
REACH = 4
F32 = jnp.float32
BF16 = jnp.bfloat16


def half_kernel(
    peers, ranks, live, lengths, coeffs, weights, ao, out,
    mine, coefs, got, held, diagonal, wide_own, high_own, direct, turned_sum, mirror, own, sent, came,
    total, padded, sheet, slabs,
    x_send, x_recv, x_own, held_sem, mine_sem, gz_send, gz_recv, gx_send, gx_recv, gy_send, gy_recv,
    gc_send, gc_recv, bx_send, bx_recv, bz_send, bz_recv, bc_send, bc_recv,
    send_sem, recv_sem, plane_send, plane_recv, line_send, line_recv,
):
    me, aux = lax.axis_index("pair"), lax.axis_index("aux")
    plane, slot = me // peers, me % peers
    chips = peers // 2
    chip, core = slot // 2, slot % 2
    slab, half, size = got.shape[2:]
    occ = mine.shape[0]
    low_rows = quarter_rows(occ, ranks)
    rest = pl.ds(low_rows * ranks, occ - low_rows * ranks)
    chunk = occ // PLANES
    share = chunk // peers
    begin = 5

    def remote(src, dst, sends, recvs, device):
        return pltpu.make_async_remote_copy(
            src_ref=src, dst_ref=dst, send_sem=sends, recv_sem=recvs,
            device_id=device, device_id_type=MESH,
        )

    def shifted(move):
        return lax.rem(plane + move + PLANES, PLANES)

    def in_plane(step):
        return lax.rem(slot + step, peers)

    def in_line(step):
        return lax.rem(aux + step + ranks, ranks)

    def in_row(step):
        return lax.rem(chip + step + chips, chips)

    def quarter(rank):
        return pl.ds(pl.multiple_of(rank * low_rows, 16), low_rows)

    def gather_z(step):
        return remote(
            mine.at[quarter(aux)], coefs.at[plane, core, chip, quarter(aux)],
            gz_send.at[step], gz_recv.at[step], (shifted(step) * peers + slot, aux),
        )

    def batch(step, rank):
        return coefs.at[:, core, in_row(-step), quarter(rank)]

    def gather_x(step):
        return remote(
            batch(0, aux), batch(0, aux), gx_send.at[step], gx_recv.at[step],
            (plane * peers + in_row(step) * 2 + core, aux),
        )

    def gather_y(step, leg):
        way = 1 if leg == 0 or (leg == 2 and step % 2 == 0) else -1
        rank = aux if leg < 2 else in_line(-way)
        return remote(
            batch(step, rank), batch(step, rank), gy_send.at[step, leg], gy_recv.at[step, leg],
            (me, in_line(way)),
        )

    other_core = (me + 1 - 2 * core, aux)

    def gather_core(step, leg):
        rank = in_line((0, -1, 1, 2)[leg])
        return remote(
            batch(step, rank), batch(step, rank), gc_send.at[step, leg], gc_recv.at[step, leg],
            other_core,
        )

    def rest_x(step):
        return remote(
            mine.at[rest], coefs.at[plane, core, chip, rest], bx_send.at[step], bx_recv.at[step],
            (plane * peers + in_row(step) * 2 + core, aux),
        )

    def ways(count, step):
        return (0, 1) if count < REACH else ((0,) if step < chips // 2 else (1,))

    def rest_z(way, count, step):
        sign = 1 if way == 0 else -1
        part = coefs.at[shifted(-sign * (count - 1)), core, in_row(-step), rest]
        return remote(
            part, part, bz_send.at[way, count - 1, step], bz_recv.at[way, count - 1, step],
            (shifted(sign) * peers + slot, aux),
        )

    def rest_core(move, step):
        part = coefs.at[shifted(move), core, in_row(-step), rest]
        spot = move + REACH - 1
        return remote(part, part, bc_send.at[spot, step], bc_recv.at[spot, step], other_core)

    own_quarter = pltpu.make_async_copy(
        mine.at[quarter(aux)], coefs.at[plane, core, chip, quarter(aux)], mine_sem.at[0]
    )
    own_rest = pltpu.make_async_copy(
        mine.at[rest], coefs.at[plane, core, chip, rest], mine_sem.at[1]
    )

    def piece(tile):
        start = pl.multiple_of(jnp.where(tile > me, 0, half), half)
        return ao.at[tile, 0, :, pl.ds(start, half), :]

    def send(group, step):
        other = in_plane(step)
        return remote(
            piece(group * peers + other), got.at[group, slot],
            x_send.at[group, step], x_recv.at[group, step], (plane * peers + other, aux),
        )

    def keep(group):
        return pltpu.make_async_copy(
            piece(group * peers + slot), got.at[group, slot], x_own.at[group]
        )

    def hold(group, m):
        return pltpu.make_async_copy(
            piece(group * peers + m), held.at[group, m], held_sem.at[group, m]
        )

    hold_diagonal = pltpu.make_async_copy(ao.at[me, 0], diagonal, mine_sem.at[2])

    def hop(way, group, left):
        halves = pl.ds(way, 1) if left == REACH else pl.ds(0, 2)
        return remote(
            sent.at[way, group, left - 1, halves], came.at[way, group, left - 1, halves],
            send_sem.at[way, group, left - 1], recv_sem.at[way, group, left - 1],
            (shifted(1 if way == 0 else -1) * peers + slot, aux),
        )

    def spread(group, step):
        other = in_plane(step)
        return remote(
            sheet.at[group, other], slabs.at[group, aux, slot],
            plane_send.at[group, step], plane_recv.at[group, step], (plane * peers + other, aux),
        )

    def line(group, step):
        return remote(
            slabs.at[group, aux], slabs.at[group, aux],
            line_send.at[group, step], line_recv.at[group, step], (me, in_line(step)),
        )

    barrier = pltpu.get_barrier_semaphore()

    def greet(device):
        pl.semaphore_signal(barrier, inc=1, device_id=device, device_id_type=MESH)

    for step in range(1, peers):
        greet((plane * peers + in_plane(step), aux))
    for step in range(1, PLANES):
        greet((shifted(step) * peers + slot, aux))
    for step in range(1, ranks):
        greet((me, in_line(step)))

    hold_diagonal.start()

    @pl.loop(0, PLANES)
    def _(group):
        for m in range(peers):
            hold(group, m).start()

    column = lax.broadcasted_iota(jnp.int32, (occ, size), 1)
    valid = jnp.where(column < lengths[me], 1.0, 0.0).astype(F32)
    mine[...] = (coeffs[...].astype(F32) * valid).astype(BF16)
    padded[...] = jnp.zeros_like(padded)
    pl.semaphore_wait(barrier, peers - 1 + PLANES - 1 + ranks - 1)

    own_quarter.start()
    own_rest.start()
    for step in range(1, chips):
        rest_x(step).start()
    for step in range(1, PLANES):
        gather_z(step).start()

    def offer(step):
        gather_y(step, 0).start()
        gather_y(step, 1).start()
        gather_core(step, 0).start()

    def relay(step):
        gather_y(step, 0).wait_recv()
        gather_y(step, 1).wait_recv()
        gather_y(step, 2).start()
        gather_core(step, 1).start()
        gather_core(step, 2).start()

    def close(step):
        gather_y(step, 2).wait_recv()
        gather_core(step, 3).start()

    def rest_next(count, step):
        for way in ways(count, step):
            rest_z(way, count, step).wait_recv()
        for way in range(2):
            if count < REACH and way in ways(count + 1, step):
                rest_z(way, count + 1, step).start()
        if count < REACH:
            rest_core(-count, step).start()
            rest_core(count, step).start()
        else:
            rest_core(REACH, step).start()

    def rest_first(step):
        if step > 0:
            rest_x(step).wait_recv()
        rest_z(0, 1, step).start()
        rest_z(1, 1, step).start()
        rest_core(0, step).start()

    def gather_turn(turn):
        @pl.when(turn == 0)
        def _():
            own_rest.wait()
            rest_first(0)
            own_quarter.wait()
            for step in range(1, PLANES):
                gather_z(step).wait_recv()
            for step in range(1, chips):
                gather_x(step).start()
            offer(0)
            rest_next(1, 0)
            for step in range(1, chips):
                rest_first(step)
            rest_next(2, 0)
            relay(0)

        @pl.when(turn == 1)
        def _():
            for step in range(1, chips):
                rest_next(1, step)
            for step in range(1, chips):
                gather_x(step).wait_recv()
                offer(step)

        @pl.when(turn == 2)
        def _():
            rest_next(3, 0)
            close(0)
            for step in range(1, chips):
                rest_next(2, step)

        @pl.when(turn == 3)
        def _():
            rest_next(REACH, 0)
            for step in range(1, chips):
                relay(step)
            for step in range(1, chips):
                rest_next(3, step)

        @pl.when(turn == 4)
        def _():
            for step in range(1, chips):
                rest_next(REACH, step)
            for step in range(1, chips):
                close(step)
            for step in range(chips):
                for leg in range(4):
                    gather_core(step, leg).wait_recv()
                for move in range(1 - REACH, REACH + 1):
                    rest_core(move, step).wait_recv()

    def one(cond):
        return jnp.where(cond, 1.0, 0.0).astype(F32)

    def kept(first, second):
        return one(live[jnp.maximum(first, second), jnp.minimum(first, second)] > 0)

    def coef(group, m):
        return coefs[group, m % 2, m // 2]

    def wide(group):
        return jnp.concatenate([coef(group, m) for m in range(peers)], axis=1)

    def cut(group, start):
        return jnp.concatenate(
            [coef(group, m)[:, start : start + half] for m in range(peers)], axis=1
        )

    def straight(left, right):
        return lax.dot_general(left, right, (((1,), (0,)), ((), ())), preferred_element_type=F32)

    def turned(left, right):
        return lax.dot_general(left, right, (((1,), (1,)), ((), ())), preferred_element_type=F32)

    def scaled(block, factor):
        return block * jnp.full((half, size), factor, F32).astype(BF16)

    lower = lax.broadcasted_iota(jnp.int32, (occ, size), 1) < half

    def place(acc, result, upper):
        for p in range(slab):
            value = result[:, (p // 2) * size : (p // 2 + 1) * size]
            if (p % 2 == 0) == upper:
                value = pltpu.roll(value, half, 1)
            value = jnp.where(lower, 0.0, value) if upper else jnp.where(lower, value, 0.0)
            acc[:, p * size : (p + 1) * size] += value

    def stacked(source, group, factors):
        return jnp.concatenate(
            [
                jnp.concatenate([scaled(source[group, m, p], factors[m]) for p in range(slab)], axis=1)
                for m in range(peers)
            ],
            axis=0,
        )

    def beside(source, group, factors):
        return jnp.concatenate(
            [
                jnp.concatenate([scaled(source[group, m, p], factors[m]) for p in range(slab)], axis=0)
                for m in range(peers)
            ],
            axis=1,
        )

    def sum_direct():
        hold_diagonal.wait()
        row = lax.broadcasted_iota(jnp.int32, (size, size), 0)
        col = lax.broadcasted_iota(jnp.int32, (size, size), 1)
        factor = kept(me, me)
        tril = (factor * one(row >= col)).astype(BF16)
        strict = (factor * one(row > col)).astype(BF16)
        blocks = [diagonal[p] * tril for p in range(slab)]
        direct[...] = straight(mine[...], jnp.concatenate(blocks, axis=1))
        blocks = [diagonal[p] * strict for p in range(slab)]
        direct[...] += turned(mine[...], jnp.concatenate(blocks, axis=0))

        turned_sum[...] = jnp.zeros_like(turned_sum)

        @pl.loop(0, PLANES)
        def _(group):
            for m in range(peers):
                hold(group, m).wait()

            @pl.when(group >= plane)
            def _():
                tiles = [group * peers + m for m in range(peers)]
                factors = [kept(tile, me) * one(tile > me) for tile in tiles]
                direct[...] += straight(cut(group, 0), stacked(held, group, factors))

            @pl.when(group <= plane)
            def _():
                tiles = [group * peers + m for m in range(peers)]
                factors = [kept(tile, me) * one(tile < me) for tile in tiles]
                turned_sum[...] += turned(wide(group), beside(held, group, factors))

        place(direct, turned_sum[...], True)

    def sum_mirror(group):
        keep(group).wait()
        for step in range(1, peers):
            send(group, step).wait_recv()
        target = group * peers + slot
        tiles = [plane * peers + m for m in range(peers)]

        @pl.when(group == plane)
        def _():
            mirror[...] = direct[...]

        @pl.when(group != plane)
        def _():
            mirror[...] = jnp.zeros_like(mirror)

        @pl.when(group >= plane)
        def _():
            factors = [kept(tile, target) * one(tile < target) for tile in tiles]
            place(mirror, turned(wide_own[...], beside(got, group, factors)), False)

        @pl.when(group <= plane)
        def _():
            factors = [kept(tile, target) * one(tile > target) for tile in tiles]
            mirror[...] += straight(high_own[...], stacked(got, group, factors))

        for z in range(PLANES):
            for p in range(slab):
                own[group, z, p // 2, (p % 2) * chunk : (p % 2 + 1) * chunk, :] = mirror[
                    z * chunk : (z + 1) * chunk, p * size : (p + 1) * size
                ]

    def pass_on(group, left):
        for way in range(2):
            goal = shifted(left if way == 0 else -left)
            if left == REACH:
                sent[way, group, left - 1, way] = own[group, goal, way].astype(BF16)
            else:
                hop(way, group, left + 1).wait_recv()
                for part in range(2):
                    value = own[group, goal, part]
                    if left < REACH - 1 or part == way:
                        value = value + came[way, group, left, part].astype(F32)
                    sent[way, group, left - 1, part] = value.astype(BF16)
            hop(way, group, left).start()

    def finish(group):
        for way in range(2):
            hop(way, group, 1).wait_recv()
        for part in range(2):
            total[part] = (
                own[group, plane, part]
                + came[0, group, 0, part].astype(F32)
                + came[1, group, 0, part].astype(F32)
            )
        for other in range(peers):
            for part in range(2):
                for odd in range(2):
                    start = odd * chunk + other * share
                    spot = (part * 2 + odd) * share
                    padded[other, spot : spot + share, :] = total[part, start : start + share, :]
            sheet[group, other] = padded[other].astype(BF16)
        slabs[group, aux, slot] = sheet[group, slot]
        for step in range(1, peers):
            spread(group, step).start()

    def along(group):
        for step in range(1, peers):
            spread(group, step).wait_recv()
        for step in range(1, ranks):
            line(group, step).start()

    inside = lax.broadcasted_iota(jnp.int32, (1, size), 1)
    panel = out.shape[1]

    def fit(group):
        for step in range(1, ranks):
            line(group, step).wait_recv()
        blocks = [
            jnp.concatenate([slabs[group, r, m] for r in range(ranks)], axis=0)
            for m in range(peers)
        ]
        result = straight(weights[...], jnp.concatenate(blocks, axis=1))
        for m in range(peers):
            valid = jnp.broadcast_to(inside < lengths[group * peers + m], (panel, size))
            columns = pl.ds(pl.multiple_of((group * peers + m) * size, size), size)
            for i in range(share):
                value = result[panel * i : panel * (i + 1), m * size : (m + 1) * size]
                out[i, :, columns] = jnp.where(valid, value, 0.0).astype(BF16)

    @pl.loop(0, begin + PLANES + REACH + 4)
    def _(turn):
        gather_turn(turn)

        @pl.when(turn == begin)
        def _():
            wide_own[...] = wide(plane)
            high_own[...] = cut(plane, half)
            sum_direct()
            sum_mirror(0)

        for left in range(REACH, 0, -1):
            group = turn - begin - (REACH - left)

            @pl.when((group >= 0) & (group < PLANES))
            def _(group=group, left=left):
                pass_on(group, left)

        @pl.when((turn >= 1) & (turn <= PLANES))
        def _():
            keep(turn - 1).start()
            for step in range(1, peers):
                send(turn - 1, step).start()

        group = turn - begin - REACH

        @pl.when((group >= 0) & (group < PLANES))
        def _(group=group):
            finish(group)

        group = turn - begin - REACH - 2

        @pl.when((group >= 0) & (group < PLANES))
        def _(group=group):
            along(group)

        group = turn - begin - REACH - 4

        @pl.when((group >= 0) & (group < PLANES))
        def _(group=group):
            fit(group)

        group = turn - begin + 1

        @pl.when((group >= 1) & (group < PLANES))
        def _(group=group):
            sum_mirror(group)

        @pl.when((turn >= 4) & (turn < PLANES + 4))
        def _():
            for step in range(1, peers):
                send(turn - 4, step).wait_send()

    for step in range(1, PLANES):
        gather_z(step).wait_send()
    for step in range(1, chips):
        gather_x(step).wait_send()
        rest_x(step).wait_send()
    for step in range(chips):
        for leg in range(3):
            gather_y(step, leg).wait_send()
        for leg in range(4):
            gather_core(step, leg).wait_send()
        for move in range(1 - REACH, REACH + 1):
            rest_core(move, step).wait_send()
        for count in range(1, REACH + 1):
            for way in ways(count, step):
                rest_z(way, count, step).wait_send()

    @pl.loop(0, PLANES)
    def _(group):
        for step in range(1, ranks):
            line(group, step).wait_send()
        for step in range(1, peers):
            spread(group, step).wait_send()
        for way in range(2):
            for left in range(1, REACH + 1):
                hop(way, group, left).wait_send()


def quarter_rows(occ, ranks):
    return 16 * max(1, (occ * 5 // 9) // (16 * ranks))


def fitted_panel(ao, block_live, tile_len, coeffs, weights, room, peers, ranks):
    _, _, slab, size, _ = ao.shape
    occ = coeffs.shape[0]
    chips = peers // 2
    rows = 2 * occ // PLANES
    share = occ // (PLANES * peers)
    dma = pltpu.SemaphoreType.DMA
    pieces = (PLANES, peers, slab, size // 2, size)
    hops = (2, PLANES, REACH)
    return pl.pallas_call(
        functools.partial(half_kernel, peers, ranks),
        out_shape=jax.ShapeDtypeStruct(
            (share, weights.shape[0] // share, PLANES * peers * size), BF16
        ),
        in_specs=[
            pl.BlockSpec(memory_space=pltpu.SMEM),
            pl.BlockSpec(memory_space=pltpu.SMEM),
            pl.BlockSpec(memory_space=pltpu.VMEM),
            pl.BlockSpec(memory_space=pltpu.VMEM),
            pl.BlockSpec(memory_space=pl.ANY),
        ],
        out_specs=pl.BlockSpec(memory_space=pltpu.VMEM),
        scratch_shapes=[
            pltpu.VMEM((occ, size), BF16),
            pltpu.VMEM((PLANES, 2, chips, occ, size), BF16),
            pltpu.VMEM(pieces, BF16),
            pltpu.VMEM(pieces, BF16),
            pltpu.VMEM((slab, size, size), BF16),
            pltpu.VMEM((occ, peers * size), BF16),
            pltpu.VMEM((occ, peers * size // 2), BF16),
            pltpu.VMEM((occ, slab * size), F32),
            pltpu.VMEM((occ, slab * size // 2), F32),
            pltpu.VMEM((occ, slab * size), F32),
            pltpu.VMEM((PLANES, PLANES, 2, rows, size), F32),
            pltpu.VMEM(hops + (2, rows, size), BF16),
            pltpu.VMEM(hops + (2, rows, size), BF16),
            pltpu.VMEM((2, rows, size), F32),
            pltpu.VMEM((peers, room, size), F32),
            pltpu.VMEM((PLANES, peers, room, size), BF16),
            pltpu.VMEM((PLANES, ranks, peers, room, size), BF16),
            dma((PLANES, peers)), dma((PLANES, peers)), dma((PLANES,)), dma((PLANES, peers)), dma((3,)),
            dma((PLANES,)), dma((PLANES,)), dma((chips,)), dma((chips,)),
            dma((chips, 3)), dma((chips, 3)), dma((chips, 4)), dma((chips, 4)),
            dma((chips,)), dma((chips,)), dma((2, REACH, chips)), dma((2, REACH, chips)),
            dma((2 * REACH, chips)), dma((2 * REACH, chips)),
            dma(hops), dma(hops), dma((PLANES, peers)), dma((PLANES, peers)),
            dma((PLANES, ranks)), dma((PLANES, ranks)),
        ],
        compiler_params=pltpu.CompilerParams(
            collective_id=0, has_side_effects=True, vmem_limit_bytes=60 << 20
        ),
    )(block_live, tile_len, coeffs, weights, ao)


def fit_weights(metric, ranks, share, room):
    slab, panel_all = metric.shape
    panel = panel_all // ranks
    local = lax.dynamic_slice_in_dim(metric, lax.axis_index("aux") * panel, panel, 1)
    weights = jnp.einsum(
        "pq,ij->iqpj", local.astype(F32), jnp.eye(share, dtype=F32)
    ).reshape(share * panel, ranks, slab // ranks * share)
    weights = jnp.pad(weights, ((0, 0), (0, 0), (0, room - weights.shape[2])))
    return weights.reshape(share * panel, ranks * room).astype(BF16)


def shards(ao_blocks, block_live, tile_len, coeffs, metric_panel):
    pairs, ranks = lax.axis_size("pair"), lax.axis_size("aux")
    peers = pairs // PLANES
    share = coeffs.shape[1] // pairs
    room = -(-(metric_panel.shape[0] // ranks * share) // 16) * 16
    weights = fit_weights(metric_panel, ranks, share, room)
    fitted = fitted_panel(
        ao_blocks, block_live, tile_len, jnp.transpose(coeffs), weights, room, peers, ranks
    )
    return jnp.transpose(fitted, (1, 0, 2))


def solution(mesh):
    in_specs = (P(None, "pair", "aux", None, None), P(), P(), P("pair", None), P())
    out_specs = P("aux", "pair", None)
    return jax.shard_map(shards, mesh=mesh, in_specs=in_specs, out_specs=out_specs, check_vma=False)
```

```python
import functools

import jax
import jax.numpy as jnp
from jax import lax
from jax.experimental import pallas as pl
from jax.experimental.pallas import tpu as pltpu
from jax.sharding import PartitionSpec as P

MESH = pl.DeviceIdType.MESH
PLANES = 8
REACH = 4
F32 = jnp.float32
BF16 = jnp.bfloat16


def half_kernel(
    peers, ranks, live, lengths, coeffs, weights, ao, out,
    mine, coefs, got, held, diagonal, wide_own, high_own, direct, turned_sum, mirror, own, sent, came,
    total, padded, sheet, seen, loose, wall, slabs,
    x_send, x_recv, x_own, held_sem, mine_sem, gz_send, gz_recv, gx_send, gx_recv, gy_send, gy_recv,
    gc_send, gc_recv, bx_send, bx_recv, bz_send, bz_recv, bc_send, bc_recv,
    send_sem, recv_sem, plane_send, plane_recv, line_send, line_recv,
):
    me, aux = lax.axis_index("pair"), lax.axis_index("aux")
    plane, slot = me // peers, me % peers
    chips = peers // 2
    chip, core = slot // 2, slot % 2
    slab, half, size = got.shape[2:]
    occ = mine.shape[0]
    low_rows = quarter_rows(occ, ranks)
    rest = pl.ds(low_rows * ranks, occ - low_rows * ranks)
    chunk = occ // PLANES
    share = chunk // peers
    tight = slab * share
    begin = 5

    def remote(src, dst, sends, recvs, device):
        return pltpu.make_async_remote_copy(
            src_ref=src, dst_ref=dst, send_sem=sends, recv_sem=recvs,
            device_id=device, device_id_type=MESH,
        )

    def shifted(move):
        return lax.rem(plane + move + PLANES, PLANES)

    def in_plane(step):
        return lax.rem(slot + step, peers)

    def in_line(step):
        return lax.rem(aux + step + ranks, ranks)

    def in_row(step):
        return lax.rem(chip + step + chips, chips)

    def quarter(rank):
        return pl.ds(pl.multiple_of(rank * low_rows, 16), low_rows)

    def gather_z(step):
        return remote(
            mine.at[quarter(aux)], coefs.at[plane, core, chip, quarter(aux)],
            gz_send.at[step], gz_recv.at[step], (shifted(step) * peers + slot, aux),
        )

    def batch(step, rank):
        return coefs.at[:, core, in_row(-step), quarter(rank)]

    def gather_x(step):
        return remote(
            batch(0, aux), batch(0, aux), gx_send.at[step], gx_recv.at[step],
            (plane * peers + in_row(step) * 2 + core, aux),
        )

    def gather_y(step, leg):
        way = 1 if leg == 0 or (leg == 2 and step % 2 == 0) else -1
        rank = aux if leg < 2 else in_line(-way)
        return remote(
            batch(step, rank), batch(step, rank), gy_send.at[step, leg], gy_recv.at[step, leg],
            (me, in_line(way)),
        )

    other_core = (me + 1 - 2 * core, aux)

    def gather_core(step, leg):
        rank = in_line((0, -1, 1, 2)[leg])
        return remote(
            batch(step, rank), batch(step, rank), gc_send.at[step, leg], gc_recv.at[step, leg],
            other_core,
        )

    def rest_x(step):
        return remote(
            mine.at[rest], coefs.at[plane, core, chip, rest], bx_send.at[step], bx_recv.at[step],
            (plane * peers + in_row(step) * 2 + core, aux),
        )

    def ways(count, step):
        return (0, 1) if count < REACH else ((0,) if step < chips // 2 else (1,))

    def rest_z(way, count, step):
        sign = 1 if way == 0 else -1
        part = coefs.at[shifted(-sign * (count - 1)), core, in_row(-step), rest]
        return remote(
            part, part, bz_send.at[way, count - 1, step], bz_recv.at[way, count - 1, step],
            (shifted(sign) * peers + slot, aux),
        )

    def rest_core(move, step):
        part = coefs.at[shifted(move), core, in_row(-step), rest]
        spot = move + REACH - 1
        return remote(part, part, bc_send.at[spot, step], bc_recv.at[spot, step], other_core)

    own_quarter = pltpu.make_async_copy(
        mine.at[quarter(aux)], coefs.at[plane, core, chip, quarter(aux)], mine_sem.at[0]
    )
    own_rest = pltpu.make_async_copy(
        mine.at[rest], coefs.at[plane, core, chip, rest], mine_sem.at[1]
    )

    def piece(tile):
        start = pl.multiple_of(jnp.where(tile > me, 0, half), half)
        return ao.at[tile, 0, :, pl.ds(start, half), :]

    def send(group, step):
        other = in_plane(step)
        return remote(
            piece(group * peers + other), got.at[group, slot],
            x_send.at[group, step], x_recv.at[group, step], (plane * peers + other, aux),
        )

    def keep(group):
        return pltpu.make_async_copy(
            piece(group * peers + slot), got.at[group, slot], x_own.at[group]
        )

    def hold(group, m):
        return pltpu.make_async_copy(
            piece(group * peers + m), held.at[group, m], held_sem.at[group, m]
        )

    hold_diagonal = pltpu.make_async_copy(ao.at[me, 0], diagonal, mine_sem.at[2])

    def hop(way, group, left):
        halves = pl.ds(way, 1) if left == REACH else pl.ds(0, 2)
        return remote(
            sent.at[way, group, left - 1, halves], came.at[way, group, left - 1, halves],
            send_sem.at[way, group, left - 1], recv_sem.at[way, group, left - 1],
            (shifted(1 if way == 0 else -1) * peers + slot, aux),
        )

    def spread(group, step):
        other = in_plane(step)
        return remote(
            sheet.at[group, other], seen.at[group, slot],
            plane_send.at[group, step], plane_recv.at[group, step], (plane * peers + other, aux),
        )

    def line(group, leg):
        way = 1 if leg % 2 == 0 else -1
        rank = aux if leg < 2 else in_line(-way)
        rows = slabs.shape[2]
        part = pl.ds(0, rows) if leg < 2 else pl.ds((leg - 2) * (rows // 2), rows // 2)
        return remote(
            slabs.at[group, rank, part], slabs.at[group, rank, part],
            line_send.at[group, leg], line_recv.at[group, leg], (me, in_line(way)),
        )

    barrier = pltpu.get_barrier_semaphore()

    def greet(device):
        pl.semaphore_signal(barrier, inc=1, device_id=device, device_id_type=MESH)

    for step in range(1, peers):
        greet((plane * peers + in_plane(step), aux))
    for step in range(1, PLANES):
        greet((shifted(step) * peers + slot, aux))
    for step in range(1, ranks):
        greet((me, in_line(step)))

    hold_diagonal.start()

    @pl.loop(0, PLANES)
    def _(group):
        for m in range(peers):
            hold(group, m).start()

    column = lax.broadcasted_iota(jnp.int32, (occ, size), 1)
    valid = jnp.where(column < lengths[me], 1.0, 0.0).astype(F32)
    mine[...] = (coeffs[...].astype(F32) * valid).astype(BF16)
    padded[...] = jnp.zeros_like(padded)
    pl.semaphore_wait(barrier, peers - 1 + PLANES - 1 + ranks - 1)

    own_quarter.start()
    own_rest.start()
    for step in range(1, chips):
        rest_x(step).start()
    for step in range(1, PLANES):
        gather_z(step).start()

    def offer(step):
        gather_y(step, 0).start()
        gather_y(step, 1).start()
        gather_core(step, 0).start()

    def relay(step):
        gather_y(step, 0).wait_recv()
        gather_y(step, 1).wait_recv()
        gather_y(step, 2).start()
        gather_core(step, 1).start()
        gather_core(step, 2).start()

    def close(step):
        gather_y(step, 2).wait_recv()
        gather_core(step, 3).start()

    def rest_next(count, step):
        for way in ways(count, step):
            rest_z(way, count, step).wait_recv()
        for way in range(2):
            if count < REACH and way in ways(count + 1, step):
                rest_z(way, count + 1, step).start()
        if count < REACH:
            rest_core(-count, step).start()
            rest_core(count, step).start()
        else:
            rest_core(REACH, step).start()

    def rest_first(step):
        if step > 0:
            rest_x(step).wait_recv()
        rest_z(0, 1, step).start()
        rest_z(1, 1, step).start()
        rest_core(0, step).start()

    def gather_turn(turn):
        @pl.when(turn == 0)
        def _():
            own_rest.wait()
            rest_first(0)
            own_quarter.wait()
            for step in range(1, PLANES):
                gather_z(step).wait_recv()
            for step in range(1, chips):
                gather_x(step).start()
            offer(0)
            rest_next(1, 0)
            for step in range(1, chips):
                rest_first(step)
            rest_next(2, 0)
            relay(0)

        @pl.when(turn == 1)
        def _():
            for step in range(1, chips):
                rest_next(1, step)
            for step in range(1, chips):
                gather_x(step).wait_recv()
                offer(step)

        @pl.when(turn == 2)
        def _():
            rest_next(3, 0)
            close(0)
            for step in range(1, chips):
                rest_next(2, step)

        @pl.when(turn == 3)
        def _():
            rest_next(REACH, 0)
            for step in range(1, chips):
                relay(step)
            for step in range(1, chips):
                rest_next(3, step)

        @pl.when(turn == 4)
        def _():
            for step in range(1, chips):
                rest_next(REACH, step)
            for step in range(1, chips):
                close(step)
            for step in range(chips):
                for leg in range(4):
                    gather_core(step, leg).wait_recv()
                for move in range(1 - REACH, REACH + 1):
                    rest_core(move, step).wait_recv()

    def one(cond):
        return jnp.where(cond, 1.0, 0.0).astype(F32)

    def kept(first, second):
        return one(live[jnp.maximum(first, second), jnp.minimum(first, second)] > 0)

    def coef(group, m):
        return coefs[group, m % 2, m // 2]

    def wide(group):
        return jnp.concatenate([coef(group, m) for m in range(peers)], axis=1)

    def cut(group, start):
        return jnp.concatenate(
            [coef(group, m)[:, start : start + half] for m in range(peers)], axis=1
        )

    def straight(left, right):
        return lax.dot_general(left, right, (((1,), (0,)), ((), ())), preferred_element_type=F32)

    def turned(left, right):
        return lax.dot_general(left, right, (((1,), (1,)), ((), ())), preferred_element_type=F32)

    def scaled(block, factor):
        return block * jnp.full((half, size), factor, F32).astype(BF16)

    lower = lax.broadcasted_iota(jnp.int32, (occ, size), 1) < half

    def place(acc, result, upper):
        for p in range(slab):
            value = result[:, (p // 2) * size : (p // 2 + 1) * size]
            if (p % 2 == 0) == upper:
                value = pltpu.roll(value, half, 1)
            value = jnp.where(lower, 0.0, value) if upper else jnp.where(lower, value, 0.0)
            acc[:, p * size : (p + 1) * size] += value

    def stacked(source, group, factors):
        return jnp.concatenate(
            [
                jnp.concatenate([scaled(source[group, m, p], factors[m]) for p in range(slab)], axis=1)
                for m in range(peers)
            ],
            axis=0,
        )

    def beside(source, group, factors):
        return jnp.concatenate(
            [
                jnp.concatenate([scaled(source[group, m, p], factors[m]) for p in range(slab)], axis=0)
                for m in range(peers)
            ],
            axis=1,
        )

    def sum_direct():
        hold_diagonal.wait()
        row = lax.broadcasted_iota(jnp.int32, (size, size), 0)
        col = lax.broadcasted_iota(jnp.int32, (size, size), 1)
        factor = kept(me, me)
        tril = (factor * one(row >= col)).astype(BF16)
        strict = (factor * one(row > col)).astype(BF16)
        blocks = [diagonal[p] * tril for p in range(slab)]
        direct[...] = straight(mine[...], jnp.concatenate(blocks, axis=1))
        blocks = [diagonal[p] * strict for p in range(slab)]
        direct[...] += turned(mine[...], jnp.concatenate(blocks, axis=0))

        turned_sum[...] = jnp.zeros_like(turned_sum)

        @pl.loop(0, PLANES)
        def _(group):
            for m in range(peers):
                hold(group, m).wait()

            @pl.when(group >= plane)
            def _():
                tiles = [group * peers + m for m in range(peers)]
                factors = [kept(tile, me) * one(tile > me) for tile in tiles]
                direct[...] += straight(cut(group, 0), stacked(held, group, factors))

            @pl.when(group <= plane)
            def _():
                tiles = [group * peers + m for m in range(peers)]
                factors = [kept(tile, me) * one(tile < me) for tile in tiles]
                turned_sum[...] += turned(wide(group), beside(held, group, factors))

        place(direct, turned_sum[...], True)

    def sum_mirror(group):
        keep(group).wait()
        for step in range(1, peers):
            send(group, step).wait_recv()
        target = group * peers + slot
        tiles = [plane * peers + m for m in range(peers)]

        @pl.when(group == plane)
        def _():
            mirror[...] = direct[...]

        @pl.when(group != plane)
        def _():
            mirror[...] = jnp.zeros_like(mirror)

        @pl.when(group >= plane)
        def _():
            factors = [kept(tile, target) * one(tile < target) for tile in tiles]
            place(mirror, turned(wide_own[...], beside(got, group, factors)), False)

        @pl.when(group <= plane)
        def _():
            factors = [kept(tile, target) * one(tile > target) for tile in tiles]
            mirror[...] += straight(high_own[...], stacked(got, group, factors))

        for z in range(PLANES):
            for p in range(slab):
                own[group, z, p // 2, (p % 2) * chunk : (p % 2 + 1) * chunk, :] = mirror[
                    z * chunk : (z + 1) * chunk, p * size : (p + 1) * size
                ]

    def pass_on(group, left):
        for way in range(2):
            goal = shifted(left if way == 0 else -left)
            if left == REACH:
                sent[way, group, left - 1, way] = own[group, goal, way].astype(BF16)
            else:
                hop(way, group, left + 1).wait_recv()
                for part in range(2):
                    value = own[group, goal, part]
                    if left < REACH - 1 or part == way:
                        value = value + came[way, group, left, part].astype(F32)
                    sent[way, group, left - 1, part] = value.astype(BF16)
            hop(way, group, left).start()

    def finish(group):
        for way in range(2):
            hop(way, group, 1).wait_recv()
        for part in range(2):
            total[part] = (
                own[group, plane, part]
                + came[0, group, 0, part].astype(F32)
                + came[1, group, 0, part].astype(F32)
            )
        for other in range(peers):
            for part in range(2):
                for odd in range(2):
                    start = odd * chunk + other * share
                    spot = (part * 2 + odd) * share
                    padded[other, spot : spot + share, :] = total[part, start : start + share, :]
            sheet[group, other] = padded[other].astype(BF16)
        seen[group, slot] = sheet[group, slot]
        for step in range(1, peers):
            spread(group, step).start()

    def along(group):
        for step in range(1, peers):
            spread(group, step).wait_recv()
        for m in range(peers):
            loose[m * tight : (m + 1) * tight, :] = seen[group, m].astype(F32)[:tight, :]
        slabs[group, aux] = loose[...].astype(BF16)
        line(group, 0).start()
        line(group, 1).start()

    def relay_line(group):
        for leg in range(2):
            line(group, leg).wait_recv()
        for leg in range(2, 4):
            line(group, leg).start()

    inside = lax.broadcasted_iota(jnp.int32, (1, size), 1)
    panel = out.shape[1]

    def fit(group):
        for leg in range(2, 4):
            line(group, leg).wait_recv()
        for r in range(ranks):
            loose[...] = slabs[group, r].astype(F32)
            for m in range(peers):
                wall[m, r * tight : (r + 1) * tight, :] = loose[m * tight : (m + 1) * tight, :]
        blocks = [wall[m].astype(BF16) for m in range(peers)]
        result = straight(weights[...], jnp.concatenate(blocks, axis=1))
        for m in range(peers):
            valid = jnp.broadcast_to(inside < lengths[group * peers + m], (panel, size))
            columns = pl.ds(pl.multiple_of((group * peers + m) * size, size), size)
            for i in range(share):
                value = result[panel * i : panel * (i + 1), m * size : (m + 1) * size]
                out[i, :, columns] = jnp.where(valid, value, 0.0).astype(BF16)

    @pl.loop(0, begin + PLANES + REACH + 3)
    def _(turn):
        gather_turn(turn)

        @pl.when(turn == begin)
        def _():
            wide_own[...] = wide(plane)
            high_own[...] = cut(plane, half)
            sum_direct()
            sum_mirror(0)

        for left in range(REACH, 0, -1):
            group = turn - begin - (REACH - left)

            @pl.when((group >= 0) & (group < PLANES))
            def _(group=group, left=left):
                pass_on(group, left)

        group = turn - begin - REACH

        @pl.when((group >= 0) & (group < PLANES))
        def _(group=group):
            finish(group)

        group = turn - begin - REACH - 1

        @pl.when((group >= 0) & (group < PLANES))
        def _(group=group):
            along(group)

        @pl.when((turn >= 0) & (turn < PLANES))
        def _():
            keep(turn).start()
            for step in range(1, peers):
                send(turn, step).start()

        group = turn - begin - REACH - 2

        @pl.when((group >= 0) & (group < PLANES))
        def _(group=group):
            relay_line(group)

        group = turn - begin - REACH - 3

        @pl.when((group >= 0) & (group < PLANES))
        def _(group=group):
            fit(group)

        group = turn - begin + 1

        @pl.when((group >= 1) & (group < PLANES))
        def _(group=group):
            sum_mirror(group)

        @pl.when((turn >= 4) & (turn < PLANES + 4))
        def _():
            for step in range(1, peers):
                send(turn - 4, step).wait_send()

    for step in range(1, PLANES):
        gather_z(step).wait_send()
    for step in range(1, chips):
        gather_x(step).wait_send()
        rest_x(step).wait_send()
    for step in range(chips):
        for leg in range(3):
            gather_y(step, leg).wait_send()
        for leg in range(4):
            gather_core(step, leg).wait_send()
        for move in range(1 - REACH, REACH + 1):
            rest_core(move, step).wait_send()
        for count in range(1, REACH + 1):
            for way in ways(count, step):
                rest_z(way, count, step).wait_send()

    @pl.loop(0, PLANES)
    def _(group):
        for leg in range(4):
            line(group, leg).wait_send()
        for step in range(1, peers):
            spread(group, step).wait_send()
        for way in range(2):
            for left in range(1, REACH + 1):
                hop(way, group, left).wait_send()


def quarter_rows(occ, ranks):
    return 16 * max(1, (occ * 5 // 9) // (16 * ranks))


def fitted_panel(ao, block_live, tile_len, coeffs, weights, room, peers, ranks):
    _, _, slab, size, _ = ao.shape
    occ = coeffs.shape[0]
    chips = peers // 2
    rows = 2 * occ // PLANES
    share = occ // (PLANES * peers)
    dma = pltpu.SemaphoreType.DMA
    pieces = (PLANES, peers, slab, size // 2, size)
    hops = (2, PLANES, REACH)
    return pl.pallas_call(
        functools.partial(half_kernel, peers, ranks),
        out_shape=jax.ShapeDtypeStruct(
            (share, weights.shape[0] // share, PLANES * peers * size), BF16
        ),
        in_specs=[
            pl.BlockSpec(memory_space=pltpu.SMEM),
            pl.BlockSpec(memory_space=pltpu.SMEM),
            pl.BlockSpec(memory_space=pltpu.VMEM),
            pl.BlockSpec(memory_space=pltpu.VMEM),
            pl.BlockSpec(memory_space=pl.ANY),
        ],
        out_specs=pl.BlockSpec(memory_space=pltpu.VMEM),
        scratch_shapes=[
            pltpu.VMEM((occ, size), BF16),
            pltpu.VMEM((PLANES, 2, chips, occ, size), BF16),
            pltpu.VMEM(pieces, BF16),
            pltpu.VMEM(pieces, BF16),
            pltpu.VMEM((slab, size, size), BF16),
            pltpu.VMEM((occ, peers * size), BF16),
            pltpu.VMEM((occ, peers * size // 2), BF16),
            pltpu.VMEM((occ, slab * size), F32),
            pltpu.VMEM((occ, slab * size // 2), F32),
            pltpu.VMEM((occ, slab * size), F32),
            pltpu.VMEM((PLANES, PLANES, 2, rows, size), F32),
            pltpu.VMEM(hops + (2, rows, size), BF16),
            pltpu.VMEM(hops + (2, rows, size), BF16),
            pltpu.VMEM((2, rows, size), F32),
            pltpu.VMEM((peers, room, size), F32),
            pltpu.VMEM((PLANES, peers, room, size), BF16),
            pltpu.VMEM((PLANES, peers, room, size), BF16),
            pltpu.VMEM((peers * slab * share, size), F32),
            pltpu.VMEM((peers, ranks * slab * share, size), F32),
            pltpu.VMEM((PLANES, ranks, peers * slab * share, size), BF16),
            dma((PLANES, peers)), dma((PLANES, peers)), dma((PLANES,)), dma((PLANES, peers)), dma((3,)),
            dma((PLANES,)), dma((PLANES,)), dma((chips,)), dma((chips,)),
            dma((chips, 3)), dma((chips, 3)), dma((chips, 4)), dma((chips, 4)),
            dma((chips,)), dma((chips,)), dma((2, REACH, chips)), dma((2, REACH, chips)),
            dma((2 * REACH, chips)), dma((2 * REACH, chips)),
            dma(hops), dma(hops), dma((PLANES, peers)), dma((PLANES, peers)),
            dma((PLANES, 4)), dma((PLANES, 4)),
        ],
        compiler_params=pltpu.CompilerParams(
            collective_id=0, has_side_effects=True, vmem_limit_bytes=60 << 20
        ),
    )(block_live, tile_len, coeffs, weights, ao)


def fit_weights(metric, ranks, share):
    slab, panel_all = metric.shape
    panel = panel_all // ranks
    local = lax.dynamic_slice_in_dim(metric, lax.axis_index("aux") * panel, panel, 1)
    weights = jnp.einsum("pq,ij->iqpj", local.astype(F32), jnp.eye(share, dtype=F32))
    return weights.reshape(share * panel, slab * share).astype(BF16)


def shards(ao_blocks, block_live, tile_len, coeffs, metric_panel):
    pairs, ranks = lax.axis_size("pair"), lax.axis_size("aux")
    peers = pairs // PLANES
    share = coeffs.shape[1] // pairs
    room = -(-(metric_panel.shape[0] // ranks * share) // 16) * 16
    weights = fit_weights(metric_panel, ranks, share)
    fitted = fitted_panel(
        ao_blocks, block_live, tile_len, jnp.transpose(coeffs), weights, room, peers, ranks
    )
    return jnp.transpose(fitted, (1, 0, 2))


def solution(mesh):
    in_specs = (P(None, "pair", "aux", None, None), P(), P(), P("pair", None), P())
    out_specs = P("aux", "pair", None)
    return jax.shard_map(shards, mesh=mesh, in_specs=in_specs, out_specs=out_specs, check_vma=False)
```

```python
import functools

import jax
import jax.numpy as jnp
from jax import lax
from jax.experimental import pallas as pl
from jax.experimental.pallas import tpu as pltpu
from jax.sharding import PartitionSpec as P

MESH = pl.DeviceIdType.MESH
PLANES = 8
REACH = 4
F32 = jnp.float32
BF16 = jnp.bfloat16


def half_kernel(
    peers, ranks, live, lengths, coeffs, weights, ao, out,
    mine, coefs, got, held, diagonal, wide_own, high_own, direct, turned_sum, mirror, own, sent, came,
    total, padded, sheet, seen, loose, wall, slabs,
    x_send, x_recv, x_own, held_sem, mine_sem, gz_send, gz_recv, gx_send, gx_recv, gy_send, gy_recv,
    gc_send, gc_recv, bx_send, bx_recv, bz_send, bz_recv, bc_send, bc_recv,
    send_sem, recv_sem, plane_send, plane_recv, line_send, line_recv,
):
    me, aux = lax.axis_index("pair"), lax.axis_index("aux")
    plane, slot = me // peers, me % peers
    chips = peers // 2
    chip, core = slot // 2, slot % 2
    slab, half, size = got.shape[2:]
    occ = mine.shape[0]
    low_rows = quarter_rows(occ, ranks)
    rest = pl.ds(low_rows * ranks, occ - low_rows * ranks)
    chunk = occ // PLANES
    share = chunk // peers
    tight = slab * share
    begin = 5

    def remote(src, dst, sends, recvs, device):
        return pltpu.make_async_remote_copy(
            src_ref=src, dst_ref=dst, send_sem=sends, recv_sem=recvs,
            device_id=device, device_id_type=MESH,
        )

    def shifted(move):
        return lax.rem(plane + move + PLANES, PLANES)

    def in_plane(step):
        return lax.rem(slot + step, peers)

    def in_line(step):
        return lax.rem(aux + step + ranks, ranks)

    def in_row(step):
        return lax.rem(chip + step + chips, chips)

    def quarter(rank):
        return pl.ds(pl.multiple_of(rank * low_rows, 16), low_rows)

    def gather_z(step):
        return remote(
            mine.at[quarter(aux)], coefs.at[plane, core, chip, quarter(aux)],
            gz_send.at[step], gz_recv.at[step], (shifted(step) * peers + slot, aux),
        )

    def batch(step, rank):
        return coefs.at[:, core, in_row(-step), quarter(rank)]

    def gather_x(step):
        return remote(
            batch(0, aux), batch(0, aux), gx_send.at[step], gx_recv.at[step],
            (plane * peers + in_row(step) * 2 + core, aux),
        )

    def gather_y(step, leg):
        way = 1 if leg == 0 or (leg == 2 and step % 2 == 0) else -1
        rank = aux if leg < 2 else in_line(-way)
        return remote(
            batch(step, rank), batch(step, rank), gy_send.at[step, leg], gy_recv.at[step, leg],
            (me, in_line(way)),
        )

    other_core = (me + 1 - 2 * core, aux)

    def gather_core(step, leg):
        rank = in_line((0, -1, 1, 2)[leg])
        return remote(
            batch(step, rank), batch(step, rank), gc_send.at[step, leg], gc_recv.at[step, leg],
            other_core,
        )

    def rest_x(step):
        return remote(
            mine.at[rest], coefs.at[plane, core, chip, rest], bx_send.at[step], bx_recv.at[step],
            (plane * peers + in_row(step) * 2 + core, aux),
        )

    def ways(count, step):
        return (0, 1) if count < REACH else ((0,) if step < chips // 2 else (1,))

    def rest_z(way, count, step):
        sign = 1 if way == 0 else -1
        part = coefs.at[shifted(-sign * (count - 1)), core, in_row(-step), rest]
        return remote(
            part, part, bz_send.at[way, count - 1, step], bz_recv.at[way, count - 1, step],
            (shifted(sign) * peers + slot, aux),
        )

    def rest_core(move, step):
        part = coefs.at[shifted(move), core, in_row(-step), rest]
        spot = move + REACH - 1
        return remote(part, part, bc_send.at[spot, step], bc_recv.at[spot, step], other_core)

    own_quarter = pltpu.make_async_copy(
        mine.at[quarter(aux)], coefs.at[plane, core, chip, quarter(aux)], mine_sem.at[0]
    )
    own_rest = pltpu.make_async_copy(
        mine.at[rest], coefs.at[plane, core, chip, rest], mine_sem.at[1]
    )

    def piece(tile):
        start = pl.multiple_of(jnp.where(tile > me, 0, half), half)
        return ao.at[tile, 0, :, pl.ds(start, half), :]

    def send(group, step):
        other = in_plane(step)
        return remote(
            piece(group * peers + other), got.at[group, slot],
            x_send.at[group, step], x_recv.at[group, step], (plane * peers + other, aux),
        )

    def keep(group):
        return pltpu.make_async_copy(
            piece(group * peers + slot), got.at[group, slot], x_own.at[group]
        )

    def hold(group, m):
        return pltpu.make_async_copy(
            piece(group * peers + m), held.at[group, m], held_sem.at[group, m]
        )

    hold_diagonal = pltpu.make_async_copy(ao.at[me, 0], diagonal, mine_sem.at[2])

    def hop(way, group, left):
        halves = pl.ds(way, 1) if left == REACH else pl.ds(0, 2)
        return remote(
            sent.at[way, group, left - 1, halves], came.at[way, group, left - 1, halves],
            send_sem.at[way, group, left - 1], recv_sem.at[way, group, left - 1],
            (shifted(1 if way == 0 else -1) * peers + slot, aux),
        )

    def spread(group, step):
        other = in_plane(step)
        return remote(
            sheet.at[group, other], seen.at[group, slot],
            plane_send.at[group, step], plane_recv.at[group, step], (plane * peers + other, aux),
        )

    def line(group, leg):
        way = 1 if leg % 2 == 0 else -1
        rank = aux if leg < 2 else in_line(-way)
        rows = slabs.shape[2]
        part = pl.ds(0, rows) if leg < 2 else pl.ds((leg - 2) * (rows // 2), rows // 2)
        return remote(
            slabs.at[group, rank, part], slabs.at[group, rank, part],
            line_send.at[group, leg], line_recv.at[group, leg], (me, in_line(way)),
        )

    barrier = pltpu.get_barrier_semaphore()

    def greet(device):
        pl.semaphore_signal(barrier, inc=1, device_id=device, device_id_type=MESH)

    for step in range(1, peers):
        greet((plane * peers + in_plane(step), aux))
    for step in range(1, PLANES):
        greet((shifted(step) * peers + slot, aux))
    for step in range(1, ranks):
        greet((me, in_line(step)))

    hold_diagonal.start()

    @pl.loop(0, PLANES)
    def _(group):
        for m in range(peers):
            hold(group, m).start()

    column = lax.broadcasted_iota(jnp.int32, (occ, size), 1)
    valid = jnp.where(column < lengths[me], 1.0, 0.0).astype(F32)
    mine[...] = (coeffs[...].astype(F32) * valid).astype(BF16)
    padded[...] = jnp.zeros_like(padded)
    pl.semaphore_wait(barrier, peers - 1 + PLANES - 1 + ranks - 1)

    own_quarter.start()
    own_rest.start()
    for step in range(1, chips):
        rest_x(step).start()
    for step in range(1, PLANES):
        gather_z(step).start()

    def offer(step):
        gather_y(step, 0).start()
        gather_y(step, 1).start()
        gather_core(step, 0).start()

    def relay(step):
        gather_y(step, 0).wait_recv()
        gather_y(step, 1).wait_recv()
        gather_y(step, 2).start()
        gather_core(step, 1).start()
        gather_core(step, 2).start()

    def close(step):
        gather_y(step, 2).wait_recv()
        gather_core(step, 3).start()

    def rest_next(count, step):
        for way in ways(count, step):
            rest_z(way, count, step).wait_recv()
        for way in range(2):
            if count < REACH and way in ways(count + 1, step):
                rest_z(way, count + 1, step).start()
        if count < REACH:
            rest_core(-count, step).start()
            rest_core(count, step).start()
        else:
            rest_core(REACH, step).start()

    def rest_first(step):
        if step > 0:
            rest_x(step).wait_recv()
        rest_z(0, 1, step).start()
        rest_z(1, 1, step).start()
        rest_core(0, step).start()

    def gather_turn(turn):
        @pl.when(turn == 0)
        def _():
            own_rest.wait()
            rest_first(0)
            own_quarter.wait()
            for step in range(1, PLANES):
                gather_z(step).wait_recv()
            for step in range(1, chips):
                gather_x(step).start()
            offer(0)
            keep(0).start()
            for step in range(1, peers):
                send(0, step).start()
            rest_next(1, 0)
            for step in range(1, chips):
                rest_first(step)
            rest_next(2, 0)
            relay(0)

        @pl.when(turn == 1)
        def _():
            for step in range(1, chips):
                rest_next(1, step)
            for step in range(1, chips):
                gather_x(step).wait_recv()
                offer(step)

        @pl.when(turn == 2)
        def _():
            rest_next(3, 0)
            close(0)
            for step in range(1, chips):
                rest_next(2, step)

        @pl.when(turn == 3)
        def _():
            rest_next(REACH, 0)
            for step in range(1, chips):
                relay(step)
            for step in range(1, chips):
                rest_next(3, step)

        @pl.when(turn == 4)
        def _():
            for step in range(1, chips):
                rest_next(REACH, step)
            for step in range(1, chips):
                close(step)
            for step in range(chips):
                for leg in range(4):
                    gather_core(step, leg).wait_recv()
                for move in range(1 - REACH, REACH + 1):
                    rest_core(move, step).wait_recv()

    def one(cond):
        return jnp.where(cond, 1.0, 0.0).astype(F32)

    def kept(first, second):
        return one(live[jnp.maximum(first, second), jnp.minimum(first, second)] > 0)

    def coef(group, m):
        return coefs[group, m % 2, m // 2]

    def wide(group):
        return jnp.concatenate([coef(group, m) for m in range(peers)], axis=1)

    def cut(group, start):
        return jnp.concatenate(
            [coef(group, m)[:, start : start + half] for m in range(peers)], axis=1
        )

    def straight(left, right):
        return lax.dot_general(left, right, (((1,), (0,)), ((), ())), preferred_element_type=F32)

    def turned(left, right):
        return lax.dot_general(left, right, (((1,), (1,)), ((), ())), preferred_element_type=F32)

    def scaled(block, factor):
        return block * jnp.full((half, size), factor, F32).astype(BF16)

    lower = lax.broadcasted_iota(jnp.int32, (occ, size), 1) < half

    def place(acc, result, upper):
        for p in range(slab):
            value = result[:, (p // 2) * size : (p // 2 + 1) * size]
            if (p % 2 == 0) == upper:
                value = pltpu.roll(value, half, 1)
            value = jnp.where(lower, 0.0, value) if upper else jnp.where(lower, value, 0.0)
            acc[:, p * size : (p + 1) * size] += value

    def stacked(source, group, factors):
        return jnp.concatenate(
            [
                jnp.concatenate([scaled(source[group, m, p], factors[m]) for p in range(slab)], axis=1)
                for m in range(peers)
            ],
            axis=0,
        )

    def beside(source, group, factors):
        return jnp.concatenate(
            [
                jnp.concatenate([scaled(source[group, m, p], factors[m]) for p in range(slab)], axis=0)
                for m in range(peers)
            ],
            axis=1,
        )

    def sum_direct():
        hold_diagonal.wait()
        row = lax.broadcasted_iota(jnp.int32, (size, size), 0)
        col = lax.broadcasted_iota(jnp.int32, (size, size), 1)
        factor = kept(me, me)
        tril = (factor * one(row >= col)).astype(BF16)
        strict = (factor * one(row > col)).astype(BF16)
        blocks = [diagonal[p] * tril for p in range(slab)]
        direct[...] = straight(mine[...], jnp.concatenate(blocks, axis=1))
        blocks = [diagonal[p] * strict for p in range(slab)]
        direct[...] += turned(mine[...], jnp.concatenate(blocks, axis=0))

        turned_sum[...] = jnp.zeros_like(turned_sum)

        @pl.loop(0, PLANES)
        def _(group):
            for m in range(peers):
                hold(group, m).wait()

            @pl.when(group >= plane)
            def _():
                tiles = [group * peers + m for m in range(peers)]
                factors = [kept(tile, me) * one(tile > me) for tile in tiles]
                direct[...] += straight(cut(group, 0), stacked(held, group, factors))

            @pl.when(group <= plane)
            def _():
                tiles = [group * peers + m for m in range(peers)]
                factors = [kept(tile, me) * one(tile < me) for tile in tiles]
                turned_sum[...] += turned(wide(group), beside(held, group, factors))

        place(direct, turned_sum[...], True)

    def sum_mirror(group):
        keep(group).wait()
        for step in range(1, peers):
            send(group, step).wait_recv()
        target = group * peers + slot
        tiles = [plane * peers + m for m in range(peers)]

        @pl.when(group == plane)
        def _():
            mirror[...] = direct[...]

        @pl.when(group != plane)
        def _():
            mirror[...] = jnp.zeros_like(mirror)

        @pl.when(group >= plane)
        def _():
            factors = [kept(tile, target) * one(tile < target) for tile in tiles]
            place(mirror, turned(wide_own[...], beside(got, group, factors)), False)

        @pl.when(group <= plane)
        def _():
            factors = [kept(tile, target) * one(tile > target) for tile in tiles]
            mirror[...] += straight(high_own[...], stacked(got, group, factors))

        for z in range(PLANES):
            for p in range(slab):
                own[group, z, p // 2, (p % 2) * chunk : (p % 2 + 1) * chunk, :] = mirror[
                    z * chunk : (z + 1) * chunk, p * size : (p + 1) * size
                ]

    def pass_on(group, left):
        for way in range(2):
            goal = shifted(left if way == 0 else -left)
            if left == REACH:
                sent[way, group, left - 1, way] = own[group, goal, way].astype(BF16)
            else:
                hop(way, group, left + 1).wait_recv()
                for part in range(2):
                    value = own[group, goal, part]
                    if left < REACH - 1 or part == way:
                        value = value + came[way, group, left, part].astype(F32)
                    sent[way, group, left - 1, part] = value.astype(BF16)
            hop(way, group, left).start()

    def finish(group):
        for way in range(2):
            hop(way, group, 1).wait_recv()
        for part in range(2):
            total[part] = (
                own[group, plane, part]
                + came[0, group, 0, part].astype(F32)
                + came[1, group, 0, part].astype(F32)
            )
        for other in range(peers):
            for part in range(2):
                for odd in range(2):
                    start = odd * chunk + other * share
                    spot = (part * 2 + odd) * share
                    padded[other, spot : spot + share, :] = total[part, start : start + share, :]
            sheet[group, other] = padded[other].astype(BF16)
        seen[group, slot] = sheet[group, slot]
        for step in range(1, peers):
            spread(group, step).start()

    def along(group):
        for step in range(1, peers):
            spread(group, step).wait_recv()
        for m in range(peers):
            loose[m * tight : (m + 1) * tight, :] = seen[group, m].astype(F32)[:tight, :]
        slabs[group, aux] = loose[...].astype(BF16)
        line(group, 0).start()
        line(group, 1).start()

    def relay_line(group):
        for leg in range(2):
            line(group, leg).wait_recv()
        for leg in range(2, 4):
            line(group, leg).start()

    inside = lax.broadcasted_iota(jnp.int32, (1, size), 1)
    panel = out.shape[1]

    def fit(group):
        for leg in range(2, 4):
            line(group, leg).wait_recv()
        for r in range(ranks):
            loose[...] = slabs[group, r].astype(F32)
            for m in range(peers):
                wall[m, r * tight : (r + 1) * tight, :] = loose[m * tight : (m + 1) * tight, :]
        blocks = [wall[m].astype(BF16) for m in range(peers)]
        result = straight(weights[...], jnp.concatenate(blocks, axis=1))
        for m in range(peers):
            valid = jnp.broadcast_to(inside < lengths[group * peers + m], (panel, size))
            columns = pl.ds(pl.multiple_of((group * peers + m) * size, size), size)
            for i in range(share):
                value = result[panel * i : panel * (i + 1), m * size : (m + 1) * size]
                out[i, :, columns] = jnp.where(valid, value, 0.0).astype(BF16)

    @pl.loop(0, begin + PLANES + REACH + 3)
    def _(turn):
        gather_turn(turn)

        @pl.when(turn == begin)
        def _():
            wide_own[...] = wide(plane)
            high_own[...] = cut(plane, half)
            sum_direct()
            sum_mirror(0)

        for left in range(REACH, 0, -1):
            group = turn - begin - (REACH - left)

            @pl.when((group >= 0) & (group < PLANES))
            def _(group=group, left=left):
                pass_on(group, left)

        group = turn - begin - REACH

        @pl.when((group >= 0) & (group < PLANES))
        def _(group=group):
            finish(group)

        group = turn - begin - REACH - 1

        @pl.when((group >= 0) & (group < PLANES))
        def _(group=group):
            along(group)

        @pl.when(turn < PLANES - 1)
        def _():
            keep(turn + 1).start()
            for step in range(1, peers):
                send(turn + 1, step).start()

        group = turn - begin - REACH - 2

        @pl.when((group >= 0) & (group < PLANES))
        def _(group=group):
            relay_line(group)

        group = turn - begin - REACH - 3

        @pl.when((group >= 0) & (group < PLANES))
        def _(group=group):
            fit(group)

        group = turn - begin + 1

        @pl.when((group >= 1) & (group < PLANES))
        def _(group=group):
            sum_mirror(group)

        @pl.when((turn >= 4) & (turn < PLANES + 4))
        def _():
            for step in range(1, peers):
                send(turn - 4, step).wait_send()

    for step in range(1, PLANES):
        gather_z(step).wait_send()
    for step in range(1, chips):
        gather_x(step).wait_send()
        rest_x(step).wait_send()
    for step in range(chips):
        for leg in range(3):
            gather_y(step, leg).wait_send()
        for leg in range(4):
            gather_core(step, leg).wait_send()
        for move in range(1 - REACH, REACH + 1):
            rest_core(move, step).wait_send()
        for count in range(1, REACH + 1):
            for way in ways(count, step):
                rest_z(way, count, step).wait_send()

    @pl.loop(0, PLANES)
    def _(group):
        for leg in range(4):
            line(group, leg).wait_send()
        for step in range(1, peers):
            spread(group, step).wait_send()
        for way in range(2):
            for left in range(1, REACH + 1):
                hop(way, group, left).wait_send()


def quarter_rows(occ, ranks):
    return 16 * max(1, (occ * 5 // 9) // (16 * ranks))


def fitted_panel(ao, block_live, tile_len, coeffs, weights, room, peers, ranks):
    _, _, slab, size, _ = ao.shape
    occ = coeffs.shape[0]
    chips = peers // 2
    rows = 2 * occ // PLANES
    share = occ // (PLANES * peers)
    dma = pltpu.SemaphoreType.DMA
    pieces = (PLANES, peers, slab, size // 2, size)
    hops = (2, PLANES, REACH)
    return pl.pallas_call(
        functools.partial(half_kernel, peers, ranks),
        out_shape=jax.ShapeDtypeStruct(
            (share, weights.shape[0] // share, PLANES * peers * size), BF16
        ),
        in_specs=[
            pl.BlockSpec(memory_space=pltpu.SMEM),
            pl.BlockSpec(memory_space=pltpu.SMEM),
            pl.BlockSpec(memory_space=pltpu.VMEM),
            pl.BlockSpec(memory_space=pltpu.VMEM),
            pl.BlockSpec(memory_space=pl.ANY),
        ],
        out_specs=pl.BlockSpec(memory_space=pltpu.VMEM),
        scratch_shapes=[
            pltpu.VMEM((occ, size), BF16),
            pltpu.VMEM((PLANES, 2, chips, occ, size), BF16),
            pltpu.VMEM(pieces, BF16),
            pltpu.VMEM(pieces, BF16),
            pltpu.VMEM((slab, size, size), BF16),
            pltpu.VMEM((occ, peers * size), BF16),
            pltpu.VMEM((occ, peers * size // 2), BF16),
            pltpu.VMEM((occ, slab * size), F32),
            pltpu.VMEM((occ, slab * size // 2), F32),
            pltpu.VMEM((occ, slab * size), F32),
            pltpu.VMEM((PLANES, PLANES, 2, rows, size), F32),
            pltpu.VMEM(hops + (2, rows, size), BF16),
            pltpu.VMEM(hops + (2, rows, size), BF16),
            pltpu.VMEM((2, rows, size), F32),
            pltpu.VMEM((peers, room, size), F32),
            pltpu.VMEM((PLANES, peers, room, size), BF16),
            pltpu.VMEM((PLANES, peers, room, size), BF16),
            pltpu.VMEM((peers * slab * share, size), F32),
            pltpu.VMEM((peers, ranks * slab * share, size), F32),
            pltpu.VMEM((PLANES, ranks, peers * slab * share, size), BF16),
            dma((PLANES, peers)), dma((PLANES, peers)), dma((PLANES,)), dma((PLANES, peers)), dma((3,)),
            dma((PLANES,)), dma((PLANES,)), dma((chips,)), dma((chips,)),
            dma((chips, 3)), dma((chips, 3)), dma((chips, 4)), dma((chips, 4)),
            dma((chips,)), dma((chips,)), dma((2, REACH, chips)), dma((2, REACH, chips)),
            dma((2 * REACH, chips)), dma((2 * REACH, chips)),
            dma(hops), dma(hops), dma((PLANES, peers)), dma((PLANES, peers)),
            dma((PLANES, 4)), dma((PLANES, 4)),
        ],
        compiler_params=pltpu.CompilerParams(
            collective_id=0, has_side_effects=True, vmem_limit_bytes=60 << 20
        ),
    )(block_live, tile_len, coeffs, weights, ao)


def fit_weights(metric, ranks, share):
    slab, panel_all = metric.shape
    panel = panel_all // ranks
    local = lax.dynamic_slice_in_dim(metric, lax.axis_index("aux") * panel, panel, 1)
    weights = jnp.einsum("pq,ij->iqpj", local.astype(F32), jnp.eye(share, dtype=F32))
    return weights.reshape(share * panel, slab * share).astype(BF16)


def shards(ao_blocks, block_live, tile_len, coeffs, metric_panel):
    pairs, ranks = lax.axis_size("pair"), lax.axis_size("aux")
    peers = pairs // PLANES
    share = coeffs.shape[1] // pairs
    room = -(-(metric_panel.shape[0] // ranks * share) // 16) * 16
    weights = fit_weights(metric_panel, ranks, share)
    fitted = fitted_panel(
        ao_blocks, block_live, tile_len, jnp.transpose(coeffs), weights, room, peers, ranks
    )
    return jnp.transpose(fitted, (1, 0, 2))


def solution(mesh):
    in_specs = (P(None, "pair", "aux", None, None), P(), P(), P("pair", None), P())
    out_specs = P("aux", "pair", None)
    return jax.shard_map(shards, mesh=mesh, in_specs=in_specs, out_specs=out_specs, check_vma=False)
```
